256 devices in a mesh: band: 128 (over z, y, x), tp: 2 (over core).
Axes of the slice: x: 4, y: 4, z: 8, core: 2. Of those that a mesh axis runs over, the one named last changes fastest.
Arguments:
- grid_input: bfloat16 [131072, 474], P('band'), may hold values from -6 to 6
- mesh_latent: bfloat16 [40960, 512], P('band'), may hold values from -6 to 6
- edge_latent: bfloat16 [327680, 512], P('band'), may hold values from -6 to 6
- slot_grid_row: int32 [384, 1024], P('band'), may hold values from 0 to 1024, as said below
- slot_mesh_row: int32 [384, 1024], P('band'), may hold values from 0 to 320, as said below
- halo_send: int32 [16384, 16], P('band'), may hold values from 0 to 320, as said below
- edge_sender: int32 [327680], P('band'), may hold values from 0 to 2367, as said below
- edge_receiver: int32 [327680], P('band'), may hold values from 0 to 319
- embed_in: bfloat16 [474, 512], P(None, 'tp'), may hold values from -0.25 to 0.25
- embed_out: bfloat16 [512, 512], P('tp'), may hold values from -0.25 to 0.25
- encode_sender: bfloat16 [512, 512], P(None, 'tp'), may hold values from -0.25 to 0.25
- encode_receiver: bfloat16 [512, 512], P(None, 'tp'), may hold values from -0.25 to 0.25
- encode_out: bfloat16 [512, 512], P('tp'), may hold values from -0.25 to 0.25
- encode_node_in: bfloat16 [1024, 512], P(None, 'tp'), may hold values from -0.1875 to 0.1875
- encode_node_out: bfloat16 [512, 512], P('tp'), may hold values from -0.25 to 0.25
- layer_sender: bfloat16 [2, 512, 512], P(None, None, 'tp'), may hold values from -0.25 to 0.25
- layer_receiver: bfloat16 [2, 512, 512], P(None, None, 'tp'), may hold values from -0.25 to 0.25
- layer_edge: bfloat16 [2, 512, 512], P(None, None, 'tp'), may hold values from -0.25 to 0.25
- layer_message: bfloat16 [2, 512, 512], P(None, 'tp'), may hold values from -0.25 to 0.25
- layer_node_in: bfloat16 [2, 1024, 512], P(None, None, 'tp'), may hold values from -0.1875 to 0.1875
- layer_node_out: bfloat16 [2, 512, 512], P(None, 'tp'), may hold values from -0.25 to 0.25
Outputs:
- mesh_result: bfloat16 [40960, 512], P('band')
The draws below stay inside these ranges and needn't reach their ends.
Inputs may be any that keep to these rules, and one draw needn't show every extreme that they name: `slot_grid_row`: 1024 marks an empty slot; live slots of a block come first; block 0 of the first band and block 2 of the last are empty; every other block holds 256 to 1024 live slots, and in every draw all three blocks sending to some partition are full. `slot_mesh_row`: 320 marks an empty slot, exactly where the matching sending slot is empty. `halo_send`: 320 marks an empty slot; live slots come first; a partition sends nothing to itself; in every draw some partition receives 16 live slots from every other. `edge_sender`: a value s at or over 320 names slot (s - 320) % 16 sent by partition (s - 320) // 16 to this one, always a live slot.
All inputs are finite; a program needn't handle non-finite values.
Results may differ from the reference program's by a relative error of at most 0.028.
Values may be sent and summed in bfloat16 or wider, within the bound.
No kernel may reach another device: no remote copies, remote signals or barrier semaphores. Data moves between devices by JAX's collectives and lax.ppermute only.
A program may use at most 64 MiB of HBM per device.

```python
import jax
import jax.numpy as jnp
from jax import lax

D = 512
HID = 512
C = 474
GRID_DEV = 1024
MESH_DEV = 320
ME_DEV = 2560
HSLOT = 16
LAYERS = 2
SLOT = 1024
GRID = 131072
MESH = 40960
MESH_EDGES = 327680
N_BAND = 128


def encoder_tables(key):
    key = jax.random.fold_in(key, 11)
    key_count, key_target, key_grid, key_mesh = jax.random.split(key, 4)
    counts = jax.random.randint(key_count, (N_BAND, 3), SLOT // 4, SLOT + 1)
    target = jax.random.randint(key_target, (), 0, N_BAND)
    device = jnp.arange(N_BAND, dtype=jnp.int32)[:, None]
    blocks = jnp.arange(3, dtype=jnp.int32)[None, :]
    counts = jnp.where(device - 1 + blocks == target, SLOT, counts)
    outside = (blocks == 0) & (device == 0) | (blocks == 2) & (device == N_BAND - 1)
    counts = jnp.where(outside, 0, counts)
    live = jnp.arange(SLOT, dtype=jnp.int32)[None, None, :] < counts[:, :, None]
    grid_rows = jnp.where(live, jax.random.randint(key_grid, (N_BAND, 3, SLOT), 0, GRID_DEV), GRID_DEV)
    mesh_rows = jnp.where(live, jax.random.randint(key_mesh, (N_BAND, 3, SLOT), 0, MESH_DEV), MESH_DEV)
    return (grid_rows.astype(jnp.int32), mesh_rows.astype(jnp.int32))


def halo_tables(key):
    key = jax.random.fold_in(key, 23)
    key_count, key_target, key_rows = jax.random.split(key, 3)
    counts = jax.random.randint(key_count, (N_BAND, N_BAND), 0, HSLOT + 1)
    target = jax.random.randint(key_target, (), 0, N_BAND)
    source = jnp.arange(N_BAND, dtype=jnp.int32)[:, None]
    dest = jnp.arange(N_BAND, dtype=jnp.int32)[None, :]
    counts = jnp.where(dest == target, HSLOT, counts)
    counts = jnp.where((source == N_BAND - 1) & (dest == 0), HSLOT, counts)
    counts = jnp.where(dest == (source + N_BAND // 2) % N_BAND, HSLOT, counts)
    counts = jnp.where(source == dest, 0, counts)
    live = jnp.arange(HSLOT, dtype=jnp.int32)[None, None, :] < counts[:, :, None]
    rows = jnp.where(live, jax.random.randint(key_rows, (N_BAND, N_BAND, HSLOT), 0, MESH_DEV), MESH_DEV)
    return (counts.astype(jnp.int32), rows.astype(jnp.int32))


def draw_slot_grid_row(key, part):
    grid_rows, mesh_rows = encoder_tables(key)
    return grid_rows.reshape(N_BAND * 3, SLOT)


def draw_slot_mesh_row(key, part):
    grid_rows, mesh_rows = encoder_tables(key)
    filler = jnp.full((1, 3, SLOT), MESH_DEV, jnp.int32)
    padded = jnp.concatenate([filler, mesh_rows, filler], axis=0)
    received = jnp.stack([padded[j:j + N_BAND, 2 - j] for j in range(3)], axis=1)
    return received.reshape(N_BAND * 3, SLOT).astype(jnp.int32)


def draw_halo_send(key, part):
    counts, rows = halo_tables(key)
    return rows.reshape(N_BAND * N_BAND, HSLOT)


def draw_edge_sender(key, part):
    counts, rows = halo_tables(key)
    key = jax.random.fold_in(key, 5)
    key_pick, key_local, key_source, key_slot = jax.random.split(key, 4)
    pick = jax.random.randint(key_pick, (N_BAND, ME_DEV), 0, 4)
    local = jax.random.randint(key_local, (N_BAND, ME_DEV), 0, MESH_DEV)
    device = jnp.arange(N_BAND, dtype=jnp.int32)[:, None]
    opposite = (device + N_BAND // 2) % N_BAND
    uniform_source = jax.random.randint(key_source, (N_BAND, ME_DEV), 0, N_BAND)
    source = jnp.where(pick <= 1, opposite, uniform_source)
    slot_pick = jax.random.randint(key_slot, (N_BAND, ME_DEV), 0, HSLOT)
    avail = counts[source, device]
    remote = (pick <= 2) & (avail > 0)
    slot_index = slot_pick % jnp.maximum(avail, 1)
    chosen = jnp.where(remote, MESH_DEV + source * HSLOT + slot_index, local)
    chosen = chosen.at[0, 0].set(MESH_DEV + N_BAND * HSLOT - 1)
    chosen = chosen.at[0, 1].set(0)
    return chosen.reshape(N_BAND * ME_DEV).astype(jnp.int32)


def place_ends(result, key, least, top_value):
    dims = result.shape
    place = [jax.random.randint(jax.random.fold_in(key, axis), (), 0, dims[axis]) for axis in range(len(dims))]
    result = result.at[tuple(place)].set(least)
    longest = dims.index(max(dims))
    place[longest] = (place[longest] + 1) % dims[longest]
    return result.at[tuple(place)].set(top_value)


def steps_of(own_key, shape, cuts, low, largest):
    def one(axis_at, shards_of):
        heights = jax.random.uniform(jax.random.fold_in(jax.random.fold_in(own_key, 6), axis_at), (shards_of,), jnp.float32, low / len(cuts), largest / len(cuts))
        return jnp.repeat(jnp.exp(heights), shape[axis_at] // shards_of).reshape((-1,) + (1,) * (len(shape) - axis_at - 1))

    gain = one(*cuts[0])
    for cut in cuts[1:]:
        gain = gain * one(*cut)
    return gain


def bell_draw(stream_key, dims, scale, bound, pieces=(), kind=jnp.bfloat16):
    entries = jax.random.normal(stream_key, dims, jnp.float32) * scale
    if len(pieces) > 0:
        entries = steps_of(stream_key, dims, pieces, -0.22, 0.18) * entries
    return jnp.clip(entries, min=-bound, max=bound).astype(kind)


def setup_inputs(seed: int = 0) -> dict:
    splits = jax.random.split(jax.random.key(seed), 22)
    return {
        "grid_input": bell_draw(splits[0], (GRID, C), 1.0, 6.0, ((0, 128),)),
        "mesh_latent": bell_draw(splits[1], (MESH, D), 1.0, 6.0, ((0, 128),)),
        "edge_latent": bell_draw(splits[2], (MESH_EDGES, D), 1.0, 6.0, ((0, 128),)),
        "slot_grid_row": draw_slot_grid_row(jax.random.fold_in(splits[21], 71), 0),
        "slot_mesh_row": draw_slot_mesh_row(jax.random.fold_in(splits[21], 71), 0),
        "halo_send": draw_halo_send(jax.random.fold_in(splits[21], 71), 0),
        "edge_sender": draw_edge_sender(jax.random.fold_in(splits[21], 71), 0),
        "edge_receiver": place_ends(jax.random.randint(splits[7], (MESH_EDGES,), 0, MESH_DEV), jax.random.fold_in(splits[7], 1), 0, MESH_DEV - 1).astype(jnp.int32),
        "embed_in": bell_draw(splits[8], (C, HID), C ** -0.5, 0.25, ((1, 2),)),
        "embed_out": bell_draw(splits[9], (HID, D), HID ** -0.5, 0.25, ((0, 2),)),
        "encode_sender": bell_draw(splits[10], (D, HID), D ** -0.5, 0.25, ((1, 2),)),
        "encode_receiver": bell_draw(splits[11], (D, HID), D ** -0.5, 0.25, ((1, 2),)),
        "encode_out": bell_draw(splits[12], (HID, D), HID ** -0.5, 0.25, ((0, 2),)),
        "encode_node_in": bell_draw(splits[13], (2 * D, HID), (2 * D) ** -0.5, 0.1875, ((1, 2),)),
        "encode_node_out": bell_draw(splits[14], (HID, D), HID ** -0.5, 0.25, ((0, 2),)),
        "layer_sender": bell_draw(splits[15], (LAYERS, D, HID), D ** -0.5, 0.25, ((2, 2),)),
        "layer_receiver": bell_draw(splits[16], (LAYERS, D, HID), D ** -0.5, 0.25, ((2, 2),)),
        "layer_edge": bell_draw(splits[17], (LAYERS, D, HID), D ** -0.5, 0.25, ((2, 2),)),
        "layer_message": bell_draw(splits[18], (LAYERS, HID, D), HID ** -0.5, 0.25, ((1, 2),)),
        "layer_node_in": bell_draw(splits[19], (LAYERS, 2 * D, HID), (2 * D) ** -0.5, 0.1875, ((2, 2),)),
        "layer_node_out": bell_draw(splits[20], (LAYERS, HID, D), HID ** -0.5, 0.25, ((1, 2),)),
    }


def normalize(values):
    centre = lax.optimization_barrier(jnp.mean(values, axis=-1, keepdims=True))
    centered = values - centre
    variance = lax.optimization_barrier(jnp.mean(centered * centered, axis=-1, keepdims=True))
    return centered * lax.rsqrt(variance + 1e-05)

def matmul(left, right):
    return jnp.dot(left, right, preferred_element_type=jnp.float32)

def rounded(values):
    return lax.optimization_barrier(values.astype(jnp.bfloat16)).astype(jnp.float32)

def node_update(latent, hidden, message_weight, first_weight, second_weight):
    message = matmul(hidden, message_weight).astype(jnp.bfloat16)
    joined = jnp.concatenate([latent, message], axis=1)
    inner = jax.nn.silu(matmul(joined, first_weight)).astype(jnp.bfloat16)
    return (latent.astype(jnp.float32) + normalize(matmul(inner, second_weight))).astype(jnp.bfloat16)

def reference(grid_input, mesh_latent, edge_latent, slot_grid_row, slot_mesh_row, halo_send, edge_sender, edge_receiver, embed_in, embed_out, encode_sender, encode_receiver, encode_out, encode_node_in, encode_node_out, layer_sender, layer_receiver, layer_edge, layer_message, layer_node_in, layer_node_out):
    bands = N_BAND
    inner = jax.nn.silu(matmul(grid_input, embed_in)).astype(jnp.bfloat16)
    grid_latent = normalize(matmul(inner, embed_out)).astype(jnp.bfloat16)
    grid_proj = matmul(grid_latent, encode_sender).astype(jnp.bfloat16)
    mesh_proj = matmul(mesh_latent, encode_receiver).astype(jnp.bfloat16)
    grid_table = slot_grid_row.reshape(bands, 3, SLOT).astype(jnp.int32)
    recv_table = slot_mesh_row.reshape(bands, 3, SLOT).astype(jnp.int32)
    filler = jnp.full((1, 3, SLOT), GRID_DEV, jnp.int32)
    padded = jnp.concatenate([filler, grid_table, filler], axis=0)
    source_rows = jnp.stack([padded[j:j + bands, 2 - j] for j in range(3)], axis=1)
    devices = jnp.arange(bands, dtype=jnp.int32)
    source_dev = devices[:, None, None] - 1 + jnp.arange(3, dtype=jnp.int32)[None, :, None]
    grid_index = jnp.clip(source_dev * GRID_DEV + source_rows, 0, bands * GRID_DEV - 1).astype(jnp.int32)

    def encode_device(inputs):
        device_grid, device_mesh, device = inputs
        flat_grid = device_grid.reshape(-1)
        flat_mesh = device_mesh.reshape(-1)
        live = flat_mesh < MESH_DEV
        local_row = jnp.minimum(flat_mesh, MESH_DEV - 1).astype(jnp.int32)
        pre_act = grid_proj[flat_grid].astype(jnp.float32) + mesh_proj[device * MESH_DEV + local_row].astype(jnp.float32)
        active = jnp.where(live[:, None], rounded(jax.nn.silu(pre_act)), jnp.float32(0.0))
        return jax.ops.segment_sum(active, local_row, num_segments=MESH_DEV)
    hidden = lax.map(encode_device, (grid_index, recv_table, devices))
    hidden = hidden.reshape(bands * MESH_DEV, HID).astype(jnp.bfloat16)
    latent = node_update(mesh_latent, hidden, encode_out, encode_node_in, encode_node_out)
    by_receiver = jnp.swapaxes(halo_send.reshape(bands, bands, HSLOT).astype(jnp.int32), 0, 1)
    senders = edge_sender.reshape(bands, ME_DEV).astype(jnp.int32)
    receivers = edge_receiver.reshape(bands, ME_DEV).astype(jnp.int32)
    edges = edge_latent.reshape(bands, ME_DEV, D)
    for layer_index in range(LAYERS):
        sender_proj = matmul(latent, layer_sender[layer_index]).astype(jnp.bfloat16)
        receiver_proj = matmul(latent, layer_receiver[layer_index]).astype(jnp.bfloat16)
        edge_weight = layer_edge[layer_index]

        def process_device(inputs, sender_proj=sender_proj, receiver_proj=receiver_proj, edge_weight=edge_weight):
            device_send, device_recv, device_edges, device_halo, device = inputs
            remote = jnp.maximum(device_send - MESH_DEV, 0)
            source = jnp.clip(remote // HSLOT, 0, bands - 1).astype(jnp.int32)
            slot_index = (remote % HSLOT).astype(jnp.int32)
            far_row = device_halo[source, slot_index]
            global_send = jnp.where(device_send < MESH_DEV, device * MESH_DEV + device_send, source * MESH_DEV + far_row).astype(jnp.int32)
            pre_act = matmul(device_edges, edge_weight) + sender_proj[global_send].astype(jnp.float32) + receiver_proj[device * MESH_DEV + device_recv].astype(jnp.float32)
            active = rounded(jax.nn.silu(pre_act))
            return jax.ops.segment_sum(active, device_recv, num_segments=MESH_DEV)
        hidden = lax.map(process_device, (senders, receivers, edges, by_receiver, devices))
        hidden = hidden.reshape(bands * MESH_DEV, HID).astype(jnp.bfloat16)
        latent = node_update(latent, hidden, layer_message[layer_index], layer_node_in[layer_index], layer_node_out[layer_index])
    return latent
```

```python
import functools

import jax
import jax.numpy as jnp
from jax import lax
from jax.experimental import pallas as pl
from jax.experimental.pallas import tpu as pltpu
from jax.sharding import PartitionSpec as P

BF16 = jnp.bfloat16
F32 = jnp.float32


def matmul(left, right):
    return jnp.dot(left, right, preferred_element_type=F32)


def silu(values):
    half = 0.5 * values
    return half + half * jnp.tanh(half)


def normalize(values):
    centre = jnp.mean(values, axis=-1, keepdims=True)
    centered = values - centre
    variance = jnp.mean(centered * centered, axis=-1, keepdims=True)
    return centered * lax.rsqrt(variance + 1e-05)


def as_column(row):
    return jnp.transpose(jnp.broadcast_to(row, (128, row.shape[1])))


def pick_rows(column, count):
    n = column.shape[0]
    wide = jnp.concatenate([column] * pl.cdiv(count, 128), axis=1)[:, :count]
    lanes = lax.broadcasted_iota(jnp.int32, (n, count), 1)
    return jnp.where(wide == lanes, 1.0, 0.0).astype(BF16)


def pick_columns(row, count):
    n = row.shape[1]
    rows = lax.broadcasted_iota(jnp.int32, (count, n), 0)
    return jnp.where(row == rows, 1.0, 0.0).astype(BF16)


def call(kernel, outs, *args):
    return pl.pallas_call(
        kernel,
        out_shape=[jax.ShapeDtypeStruct(shape, dtype) for shape, dtype in outs],
        in_specs=[pl.BlockSpec(memory_space=pltpu.VMEM)] * len(args),
        out_specs=[pl.BlockSpec(memory_space=pltpu.VMEM)] * len(outs),
        compiler_params=pltpu.CompilerParams(vmem_limit_bytes=48 * 1024 * 1024),
    )(*args)


def embed_kernel(
    x_ref, in_own, in_other, out_own, out_other, sender_w, slots, low_ref, mid_ref, high_ref
):
    rows = x_ref.shape[0]
    x = x_ref[...]
    own = silu(matmul(x, in_own[...])).astype(BF16)
    other = silu(matmul(x, in_other[...])).astype(BF16)
    total = matmul(own, out_own[...]) + matmul(other, out_other[...])
    latent = normalize(total).astype(BF16)
    proj = matmul(latent, sender_w[...]).astype(BF16)
    for block, out in enumerate((low_ref, mid_ref, high_ref)):
        index = as_column(slots[block : block + 1, :])
        out[...] = matmul(pick_rows(index, rows), proj).astype(BF16)


def join(incoming, row, mesh_proj):
    count = mesh_proj.shape[0]
    pre_act = incoming.astype(F32) + matmul(pick_rows(as_column(row), count), mesh_proj)
    return matmul(pick_columns(row, count), silu(pre_act).astype(BF16))


def encode_mid_kernel(latent, receiver_w, slots, mid, proj_ref, sum_ref):
    proj = matmul(latent[...], receiver_w[...]).astype(BF16)
    proj_ref[...] = proj
    sum_ref[...] = join(mid[...], slots[1:2, :], proj)


def encode_far_kernel(proj, partial, slots, low, high, hidden_ref):
    table = proj[...]
    total = partial[...] + join(low[...], slots[0:1, :], table)
    total = total + join(high[...], slots[2:3, :], table)
    hidden_ref[...] = total.astype(BF16)


def node_kernel(more, latent, hidden_own, hidden_other, msg_own, msg_other, first_own, first_other,
                second_own, second_other, *refs):
    width = latent.shape[1]
    message = (
        matmul(hidden_own[...], msg_own[...]) + matmul(hidden_other[...], msg_other[...])
    ).astype(BF16)
    total = None
    for first, second in ((first_own, second_own), (first_other, second_other)):
        inner = silu(matmul(latent[...], first[:width, :]) + matmul(message, first[width:, :]))
        part = matmul(inner.astype(BF16), second[...])
        total = part if total is None else total + part
    new = (latent[...].astype(F32) + normalize(total)).astype(BF16)
    if not more:
        refs[0][...] = new
        return
    sender_w, receiver_w, halo, new_ref, local_ref, receiver_ref, outgoing_ref = refs
    new_ref[...] = new
    local = matmul(new, sender_w[...]).astype(BF16)
    local_ref[...] = local
    slots = halo.shape[1]
    outgoing_ref[...] = matmul(pick_rows(as_column(halo[...]), local.shape[0]), local).astype(BF16)
    receiver_ref[...] = matmul(new, receiver_w[...]).astype(BF16)


def edge_kernel(chunk, edges, edge_w, local, arrived, receiver_proj, senders, receivers, hidden_ref):
    count = local.shape[0]
    far = arrived.shape[0]
    total = None
    for start in range(0, edges.shape[0], chunk):
        sender = senders[:, start : start + chunk]
        receiver = receivers[:, start : start + chunk]
        column = as_column(sender)
        pre_act = matmul(edges[start : start + chunk, :], edge_w[...])
        pre_act += matmul(pick_rows(column - count, far), arrived[...])
        pre_act += matmul(pick_rows(column, count), local[...])
        pre_act += matmul(pick_rows(as_column(receiver), count), receiver_proj[...])
        part = matmul(pick_columns(receiver, count), silu(pre_act).astype(BF16))
        total = part if total is None else total + part
    hidden_ref[...] = total.astype(BF16)


def swap(values):
    return lax.ppermute(values, "tp", [(0, 1), (1, 0)])


def shards(
    grid_input,
    mesh_latent,
    edge_latent,
    slot_grid_row,
    slot_mesh_row,
    halo_send,
    edge_sender,
    edge_receiver,
    embed_in,
    embed_out,
    encode_sender,
    encode_receiver,
    encode_out,
    encode_node_in,
    encode_node_out,
    layer_sender,
    layer_receiver,
    layer_edge,
    layer_message,
    layer_node_in,
    layer_node_out,
):
    nodes, width = mesh_latent.shape
    slot_count = slot_grid_row.shape[1]
    half = encode_sender.shape[1]
    bands, halo_slots = halo_send.shape
    layers = layer_sender.shape[0]
    halo_row = halo_send.reshape(1, -1)
    sender_row = edge_sender.reshape(1, -1)
    receiver_row = edge_receiver.reshape(1, -1)

    slots_out = [((slot_count, half), BF16)] * 3
    low, mid, high = call(
        embed_kernel, slots_out, grid_input, embed_in, swap(embed_in), embed_out, swap(embed_out),
        encode_sender, slot_grid_row,
    )
    up = [(i, i + 1) for i in range(bands - 1)]
    down = [(i + 1, i) for i in range(bands - 1)]
    from_low = lax.ppermute(high, "band", up)
    from_high = lax.ppermute(low, "band", down)
    proj, partial = call(
        encode_mid_kernel, [((nodes, half), BF16), ((nodes, half), F32)],
        mesh_latent, encode_receiver, slot_mesh_row, mid,
    )
    (hidden,) = call(
        encode_far_kernel, [((nodes, half), BF16)], proj, partial, slot_mesh_row, from_low, from_high
    )

    def update(latent, hidden, message, first, second, following):
        args = (latent, hidden, swap(hidden), message, swap(message), first, swap(first), second,
                swap(second))
        outs = [((nodes, width), BF16)]
        if following:
            args += following
            outs += [((nodes, half), BF16)] * 2 + [((bands * halo_slots, half), BF16)]
        return call(functools.partial(node_kernel, bool(following)), outs, *args)

    message, first, second = encode_out, encode_node_in, encode_node_out
    latent = mesh_latent
    for layer in range(layers):
        latent, local, receiver_proj, outgoing = update(
            latent, hidden, message, first, second,
            (layer_sender[layer], layer_receiver[layer], halo_row),
        )
        arrived = lax.all_to_all(
            outgoing.reshape(bands, halo_slots, half), "band", split_axis=0, concat_axis=0, tiled=True
        ).reshape(bands * halo_slots, half)
        (hidden,) = call(
            functools.partial(edge_kernel, 512), [((nodes, half), BF16)], edge_latent,
            layer_edge[layer], local, arrived, receiver_proj, sender_row, receiver_row,
        )
        message, first, second = layer_message[layer], layer_node_in[layer], layer_node_out[layer]
    (latent,) = update(latent, hidden, message, first, second, ())
    return latent


def solution(mesh):
    return jax.shard_map(
        shards,
        mesh=mesh,
        in_specs=(
            P("band", None),
            P("band", None),
            P("band", None),
            P("band", None),
            P("band", None),
            P("band", None),
            P("band"),
            P("band"),
            P(None, "tp"),
            P("tp", None),
            P(None, "tp"),
            P(None, "tp"),
            P("tp", None),
            P(None, "tp"),
            P("tp", None),
            P(None, None, "tp"),
            P(None, None, "tp"),
            P(None, None, "tp"),
            P(None, "tp", None),
            P(None, None, "tp"),
            P(None, "tp", None),
        ),
        out_specs=P("band", None),
        check_vma=False,
    )
```

```python
import functools

import jax
import jax.numpy as jnp
from jax import lax
from jax.experimental import pallas as pl
from jax.experimental.pallas import tpu as pltpu
from jax.sharding import PartitionSpec as P

BF16 = jnp.bfloat16
F32 = jnp.float32


def matmul(left, right):
    return jnp.dot(left, right, preferred_element_type=F32)


def silu(values):
    half = 0.5 * values
    return half + half * jnp.tanh(half)


def normalize(values):
    centre = jnp.mean(values, axis=-1, keepdims=True)
    centered = values - centre
    variance = jnp.mean(centered * centered, axis=-1, keepdims=True)
    return centered * lax.rsqrt(variance + 1e-05)


def as_column(row):
    return jnp.transpose(jnp.broadcast_to(row, (128, row.shape[1])))


def pick_rows(column, count):
    n = column.shape[0]
    wide = jnp.concatenate([column] * pl.cdiv(count, 128), axis=1)[:, :count]
    lanes = lax.broadcasted_iota(jnp.int32, (n, count), 1)
    return jnp.where(wide == lanes, 1.0, 0.0).astype(BF16)


def pick_columns(row, count):
    n = row.shape[1]
    rows = lax.broadcasted_iota(jnp.int32, (count, n), 0)
    return jnp.where(row == rows, 1.0, 0.0).astype(BF16)


class Layer:
    def __init__(self, array, layer):
        self.array, self.layer = array, layer


class Far:
    def __init__(self, array, layer=None, pieces=1):
        self.array, self.layer, self.pieces = array, layer, pieces
        self.shape = array.shape if layer is None else array.shape[1:]


class Incoming:
    def __init__(self, spec, ref, held, sems, first):
        source = ref if spec.layer is None else ref.at[spec.layer]
        self.held, self.shape, self.rows = held, spec.shape, spec.shape[0] // spec.pieces
        self.copies = []
        for piece in range(spec.pieces):
            rows = pl.ds(piece * self.rows, self.rows)
            self.copies.append(
                pltpu.make_async_copy(source.at[rows], held.at[rows], sems.at[first + piece])
            )
        self.waiting = [True] * spec.pieces
        for copy in self.copies:
            copy.start()

    def piece(self, index):
        if self.waiting[index]:
            self.copies[index].wait()
            self.waiting[index] = False
        return self.held[index * self.rows : (index + 1) * self.rows, :]

    def __getitem__(self, key):
        for index in range(len(self.copies)):
            self.piece(index)
        return self.held[key]


class Outgoing:
    def __init__(self, ref, held, sems, first, pieces):
        self.ref, self.held, self.sems, self.first = ref, held, sems, first
        self.rows, self.copies = ref.shape[0] // pieces, []

    def put(self, index, values):
        rows = pl.ds(index * self.rows, self.rows)
        self.held[index * self.rows : (index + 1) * self.rows, :] = values
        copy = pltpu.make_async_copy(
            self.held.at[rows], self.ref.at[rows], self.sems.at[self.first + index]
        )
        copy.start()
        self.copies.append(copy)


def call(kernel, outs, *args):
    scratch, semaphores = [], 0
    for arg in args:
        if isinstance(arg, Far):
            scratch.append(pltpu.VMEM(arg.shape, arg.array.dtype))
            semaphores += arg.pieces
    for shape, dtype, pieces in outs:
        if pieces:
            scratch.append(pltpu.VMEM(shape, dtype))
            semaphores += pieces

    def body(*refs):
        inputs, refs = refs[: len(args)], refs[len(args) :]
        results, held = refs[: len(outs)], list(refs[len(outs) : -1])
        sems, first = refs[-1], 0
        taken, given = [], []
        for arg, ref in zip(args, inputs):
            if isinstance(arg, Far):
                ref = Incoming(arg, ref, held.pop(0), sems, first)
                first += arg.pieces
            if isinstance(arg, Layer):
                ref = ref.at[arg.layer]
            taken.append(ref)
        for (shape, dtype, pieces), ref in zip(outs, results):
            if pieces:
                ref = Outgoing(ref, held.pop(0), sems, first, pieces)
                first += pieces
            given.append(ref)
        kernel(*taken, *given)
        for ref in taken:
            if isinstance(ref, Incoming):
                for index in range(len(ref.copies)):
                    if ref.waiting[index]:
                        ref.copies[index].wait()
        for ref in given:
            if isinstance(ref, Outgoing):
                for copy in ref.copies:
                    copy.wait()

    def space(far):
        return pl.BlockSpec(memory_space=pltpu.HBM if far else pltpu.VMEM)

    def operand(arg):
        if isinstance(arg, Far):
            return pltpu.with_memory_space_constraint(arg.array, pltpu.HBM)
        return arg.array if isinstance(arg, Layer) else arg

    return pl.pallas_call(
        body,
        out_shape=[
            pltpu.HBM(shape, dtype) if pieces else jax.ShapeDtypeStruct(shape, dtype)
            for shape, dtype, pieces in outs
        ],
        in_specs=[space(isinstance(arg, Far)) for arg in args],
        out_specs=[space(pieces > 0) for _, _, pieces in outs],
        scratch_shapes=scratch + [pltpu.SemaphoreType.DMA((max(semaphores, 1),))],
        compiler_params=pltpu.CompilerParams(vmem_limit_bytes=32 * 1024 * 1024),
    )(*[operand(arg) for arg in args])


def embed_kernel(blocks, features, *refs):
    inputs, refs = refs[:blocks], refs[-8:]
    in_own, in_other, out_own, out_other, sender_own, sender_other, own_ref, other_ref = refs
    rows = inputs[0].shape[0]
    for block, x_ref in enumerate(inputs):
        x = x_ref[:, :features]
        own = silu(matmul(x, in_own[...])).astype(BF16)
        other = silu(matmul(x, in_other[...])).astype(BF16)
        total = matmul(own, out_own[...]) + matmul(other, out_other[...])
        latent = normalize(total).astype(BF16)
        place = slice(block * rows, (block + 1) * rows)
        other_ref[place, :] = matmul(latent, sender_other[...]).astype(BF16)
        own_ref[place, :] = matmul(latent, sender_own[...]).astype(BF16)


def join(column, own, other, mesh_row, mesh_proj):
    rows, count = own.shape[0], mesh_proj.shape[0]
    mine = lax.axis_index("tp") * rows
    pre_act = matmul(pick_rows(column - mine, rows), own)
    pre_act += matmul(pick_rows(column - (rows - mine), rows), other)
    pre_act += matmul(pick_rows(as_column(mesh_row), count), mesh_proj)
    return matmul(pick_columns(mesh_row, count), silu(pre_act).astype(BF16))


def prepare(latent, msg_own, msg_other, first_own, first_other, base_ref, fold_ref):
    width = latent.shape[1]
    firsts = (first_own, first_other)
    base_ref.put(0, jnp.concatenate([matmul(latent, each[:width, :]) for each in firsts], axis=1))
    fold = [
        jnp.concatenate([matmul(msg[...], each[width:, :]) for each in firsts], axis=1)
        for msg in (msg_own, msg_other)
    ]
    fold_ref.put(0, jnp.concatenate(fold, axis=0).astype(BF16))


def encode_mid_kernel(latent, receiver_w, grid_slots, mesh_slots, own, other, msg_own, msg_other,
                      first_own, first_other, proj_ref, sum_ref, base_ref, fold_ref):
    nodes = latent[...]
    proj = matmul(nodes, receiver_w[...]).astype(BF16)
    proj_ref[...] = proj
    column = as_column(grid_slots[1:2, :])
    sum_ref[...] = join(column, own[...], other[...], mesh_slots[1:2, :], proj)
    prepare(nodes, msg_own, msg_other, first_own, first_other, base_ref, fold_ref)


def encode_far_kernel(features, mesh_proj, partial, mesh_slots, below, above, own, other, hidden_ref):
    table = mesh_proj[...]
    rows = below.shape[0]
    total = partial[...]
    for side, (payload, block) in enumerate(((below, 2), (above, 0))):
        place = slice(side * rows, (side + 1) * rows)
        for part in range(2):
            at = features + 2 * block + 2 * part
            digits = payload[:, at : at + 2].astype(F32)
            column = (digits[:, :1] * 32 + digits[:, 1:]).astype(jnp.int32)
            column = jnp.broadcast_to(column, (rows, 128))
            mesh_row = mesh_slots[2 - block : 3 - block, part * rows : (part + 1) * rows]
            total = total + join(column, own[place, :], other[place, :], mesh_row, table)
    hidden_ref[...] = total.astype(BF16)


def node_kernel(hidden_own, hidden_other, fold, base, second_own, second_other, latent, *refs):
    half = hidden_own.shape[1]
    pre_act = matmul(hidden_own[...], fold[:half, :]) + matmul(hidden_other[...], fold[half:, :])
    inner = silu(base[...] + pre_act).astype(BF16)
    total = matmul(inner[:, :half], second_own[...]) + matmul(inner[:, half:], second_other[...])
    new = (latent[...].astype(F32) + normalize(total)).astype(BF16)
    if len(refs) == 1:
        refs[0][...] = new
        return
    sender_w, halo, new_ref, outgoing_ref = refs
    new_ref.put(0, new)
    local = matmul(new, sender_w[...]).astype(BF16)
    column = as_column(halo[...])
    rows = outgoing_ref.rows
    for start in range(0, column.shape[0], rows):
        picked = matmul(pick_rows(column[start : start + rows, :], local.shape[0]), local)
        outgoing_ref.put(start // rows, picked.astype(BF16))


def edge_near_kernel(latent, sender_w, receiver_w, edge_w, edges, senders, receivers, msg_own,
                     msg_other, first_own, first_other, near_ref, base_ref, fold_ref):
    nodes = latent[...]
    count = nodes.shape[0]
    table = jnp.concatenate(
        [matmul(nodes, sender_w[...]).astype(BF16), matmul(nodes, receiver_w[...]).astype(BF16)],
        axis=0,
    )
    rows = near_ref.rows
    for start in range(0, edges.shape[0], rows):
        sender = as_column(senders[:, start : start + rows])
        receiver = as_column(receivers[:, start : start + rows])
        pick = jnp.concatenate([pick_rows(sender, count), pick_rows(receiver, count)], axis=1)
        near = matmul(edges.piece(start // rows), edge_w[...]) + matmul(pick, table)
        near_ref.put(start // rows, near.astype(near_ref.held.dtype))
    prepare(nodes, msg_own, msg_other, first_own, first_other, base_ref, fold_ref)


def edge_far_kernel(count, arrived, near, senders, receivers, hidden_ref):
    far = arrived.shape[0]
    rows = near.rows
    total = None
    for start in range(0, near.shape[0], rows):
        sender = as_column(senders[:, start : start + rows]) - count
        pre_act = matmul(pick_rows(sender, far), arrived[...])
        pre_act = near.piece(start // rows).astype(F32) + pre_act
        part = matmul(
            pick_columns(receivers[:, start : start + rows], count), silu(pre_act).astype(BF16)
        )
        total = part if total is None else total + part
    hidden_ref[...] = total.astype(BF16)


def swap(values):
    return lax.ppermute(values, "tp", [(0, 1), (1, 0)])


def shards(
    grid_input,
    mesh_latent,
    edge_latent,
    slot_grid_row,
    slot_mesh_row,
    halo_send,
    edge_sender,
    edge_receiver,
    embed_in,
    embed_out,
    encode_sender,
    encode_receiver,
    encode_out,
    encode_node_in,
    encode_node_out,
    layer_sender,
    layer_receiver,
    layer_edge,
    layer_message,
    layer_node_in,
    layer_node_out,
):
    nodes, width = mesh_latent.shape
    half = encode_sender.shape[1]
    bands, halo_slots = halo_send.shape
    layers = layer_sender.shape[0]
    edge_count = edge_latent.shape[0]
    pieces = 5

    rows, features = grid_input.shape[0] // 2, grid_input.shape[1]
    mine = lax.dynamic_slice_in_dim(grid_input, lax.axis_index("tp") * rows, rows, axis=0)
    digits = []
    for block in (0, 2):
        for part in range(2):
            slots = slot_grid_row[block, part * rows : (part + 1) * rows]
            digits += [slots >> 5, slots & 31]
    payload = jnp.concatenate([mine, jnp.stack(digits, axis=1).astype(BF16)], axis=1)
    below = lax.ppermute(payload, "band", [(i, i + 1) for i in range(bands - 1)])
    above = lax.ppermute(payload, "band", [(i + 1, i) for i in range(bands - 1)])

    embed_weights = (
        Far(embed_in), Far(swap(embed_in)), Far(embed_out), Far(swap(embed_out)),
        Far(encode_sender), Far(swap(encode_sender)),
    )

    def embed(blocks, *after):
        out = ((len(blocks) * rows, half), BF16, 0)
        kernel = functools.partial(embed_kernel, len(blocks), features)
        own, other = call(kernel, [out, out], *blocks, *after, *embed_weights)
        return own, swap(other)

    def prepare_weights(message, first, layer):
        return [Far(each, layer) for pair in (message, first) for each in pair]

    prepared = [((nodes, width), F32, 1), ((width, width), BF16, 1)]
    encode_message, encode_first, encode_second = [
        (each, swap(each)) for each in (encode_out, encode_node_in, encode_node_out)
    ]
    own, other = embed([payload])
    mesh_proj, partial, base, fold = call(
        encode_mid_kernel, [((nodes, half), BF16, 0), ((nodes, half), F32, 0)] + prepared,
        Far(mesh_latent), Far(encode_receiver), slot_grid_row, slot_mesh_row, own, other,
        *prepare_weights(encode_message, encode_first, None),
    )
    far_own, far_other = embed([below, above], partial)
    (hidden,) = call(
        functools.partial(encode_far_kernel, features), [((nodes, half), BF16, 0)], mesh_proj,
        partial, slot_mesh_row, below, above, far_own, far_other,
    )

    message, first, second = [
        (each, swap(each)) for each in (layer_message, layer_node_in, layer_node_out)
    ]
    halo_row = halo_send.reshape(1, -1)
    sender_row = edge_sender.reshape(1, -1)
    receiver_row = edge_receiver.reshape(1, -1)
    node_out = [((nodes, width), BF16, 1), ((bands * halo_slots, half), BF16, 4)]

    update = [Far(fold), Far(base), Far(encode_second[0]), Far(encode_second[1]), Far(mesh_latent)]
    for layer in range(layers):
        sender_w = Far(layer_sender, layer)
        latent, outgoing = call(
            node_kernel, node_out, hidden, swap(hidden), *update, sender_w, halo_row
        )
        arrived = lax.all_to_all(
            outgoing.reshape(bands, halo_slots, half), "band", split_axis=0, concat_axis=0, tiled=True
        ).reshape(bands * halo_slots, half)
        near, base, fold = call(
            edge_near_kernel, [((edge_count, half), BF16, pieces)] + prepared, Far(latent), sender_w,
            Far(layer_receiver, layer), Far(layer_edge, layer), Far(edge_latent, None, pieces),
            sender_row, receiver_row, *prepare_weights(message, first, layer),
        )
        (hidden,) = call(
            functools.partial(edge_far_kernel, nodes), [((nodes, half), BF16, 0)], arrived,
            Far(near, None, pieces), sender_row, receiver_row,
        )
        update = [fold, base, Layer(second[0], layer), Layer(second[1], layer), latent]
    (latent,) = call(node_kernel, [((nodes, width), BF16, 0)], hidden, swap(hidden), *update)
    return latent


def solution(mesh):
    return jax.shard_map(
        shards,
        mesh=mesh,
        in_specs=(
            P("band", None),
            P("band", None),
            P("band", None),
            P("band", None),
            P("band", None),
            P("band", None),
            P("band"),
            P("band"),
            P(None, "tp"),
            P("tp", None),
            P(None, "tp"),
            P(None, "tp"),
            P("tp", None),
            P(None, "tp"),
            P("tp", None),
            P(None, None, "tp"),
            P(None, None, "tp"),
            P(None, None, "tp"),
            P(None, "tp", None),
            P(None, None, "tp"),
            P(None, "tp", None),
        ),
        out_specs=P("band", None),
        check_vma=False,
    )
```

```python
import functools

import jax
import jax.numpy as jnp
from jax import lax
from jax.experimental import pallas as pl
from jax.experimental.pallas import tpu as pltpu
from jax.sharding import PartitionSpec as P

BF16 = jnp.bfloat16
F32 = jnp.float32


def matmul(left, right, left_dim=1, right_dim=0):
    dims = (((left_dim,), (right_dim,)), ((), ()))
    return lax.dot_general(left, right, dims, preferred_element_type=F32)


def silu(values):
    half = 0.5 * values
    return half + half * jnp.tanh(half)


def normalize(values, axis):
    centre = jnp.mean(values, axis=axis, keepdims=True)
    centered = values - centre
    variance = jnp.mean(centered * centered, axis=axis, keepdims=True)
    return centered * lax.rsqrt(variance + 1e-05)


def as_column(row):
    return jnp.transpose(jnp.broadcast_to(row, (128, row.shape[1])))


def pick_rows(column, count):
    n = column.shape[0]
    wide = jnp.concatenate([column] * pl.cdiv(count, 128), axis=1)[:, :count]
    lanes = lax.broadcasted_iota(jnp.int32, (n, count), 1)
    return jnp.where(wide == lanes, 1.0, 0.0).astype(BF16)


def pick_columns(row, count):
    n = row.shape[1]
    rows = lax.broadcasted_iota(jnp.int32, (count, n), 0)
    return jnp.where(row == rows, 1.0, 0.0).astype(BF16)


class Carry:
    def __init__(self, array, layer=None):
        self.array, self.layer = array, layer
        self.shape = array.shape if layer is None else array.shape[1:]


class Layer:
    def __init__(self, array, layer):
        self.array, self.layer = array, layer


class Far:
    def __init__(self, array, layer=None, pieces=1):
        self.array, self.layer, self.pieces = array, layer, pieces
        self.shape = array.shape if layer is None else array.shape[1:]


class Incoming:
    def __init__(self, spec, ref, held, sems, first):
        source = ref if spec.layer is None else ref.at[spec.layer]
        self.held, self.shape, self.rows = held, spec.shape, spec.shape[0] // spec.pieces
        self.copies = []
        for piece in range(spec.pieces):
            rows = pl.ds(piece * self.rows, self.rows)
            self.copies.append(
                pltpu.make_async_copy(source.at[rows], held.at[rows], sems.at[first + piece])
            )
        self.waiting = [True] * spec.pieces
        for copy in self.copies:
            copy.start()

    def piece(self, index):
        if self.waiting[index]:
            self.copies[index].wait()
            self.waiting[index] = False
        return self.held[index * self.rows : (index + 1) * self.rows, :]

    def __getitem__(self, key):
        for index in range(len(self.copies)):
            self.piece(index)
        return self.held[key]


class Outgoing:
    def __init__(self, ref, held, sems, first, pieces):
        self.ref, self.held, self.sems, self.first = ref, held, sems, first
        self.rows, self.copies = ref.shape[0] // pieces, []

    def put(self, index, values):
        rows = pl.ds(index * self.rows, self.rows)
        self.held[index * self.rows : (index + 1) * self.rows, :] = values
        copy = pltpu.make_async_copy(
            self.held.at[rows], self.ref.at[rows], self.sems.at[self.first + index]
        )
        copy.start()
        self.copies.append(copy)


def call(kernel, outs, *args):
    scratch, semaphores = [], 0
    for arg in args:
        if isinstance(arg, Far):
            scratch.append(pltpu.VMEM(arg.shape, arg.array.dtype))
            semaphores += arg.pieces
    for shape, dtype, pieces in outs:
        if pieces:
            scratch.append(pltpu.VMEM(shape, dtype))
            semaphores += pieces
    carried = [arg for arg in args if isinstance(arg, Carry)]
    semaphores += len(carried)
    all_outs = list(outs) + [(arg.shape, arg.array.dtype, 0) for arg in carried]

    def body(*refs):
        inputs, refs = refs[: len(args)], refs[len(args) :]
        results, held = refs[: len(all_outs)], list(refs[len(all_outs) : -1])
        sems, first = refs[-1], 0
        copied = list(results[len(outs) :])
        taken, given, carries = [], [], []
        for arg, ref in zip(args, inputs):
            if isinstance(arg, Far):
                taken.append(Incoming(arg, ref, held.pop(0), sems, first))
                first += arg.pieces
            elif isinstance(arg, Carry):
                source = ref if arg.layer is None else ref.at[arg.layer]
                carries.append(pltpu.make_async_copy(source, copied.pop(0), sems.at[first]))
                first += 1
            else:
                taken.append(ref.at[arg.layer] if isinstance(arg, Layer) else ref)
        for copy in carries:
            copy.start()
        for (shape, dtype, pieces), ref in zip(outs, results):
            if pieces:
                ref = Outgoing(ref, held.pop(0), sems, first, pieces)
                first += pieces
            given.append(ref)
        kernel(*taken, *given)
        for ref in taken:
            if isinstance(ref, Incoming):
                for index in range(len(ref.copies)):
                    if ref.waiting[index]:
                        ref.copies[index].wait()
        for ref in given:
            if isinstance(ref, Outgoing):
                for copy in ref.copies:
                    copy.wait()
        for copy in carries:
            copy.wait()

    def space(far):
        return pl.BlockSpec(memory_space=pltpu.HBM if far else pltpu.VMEM)

    def operand(arg):
        if isinstance(arg, (Far, Carry)):
            return pltpu.with_memory_space_constraint(arg.array, pltpu.HBM)
        return arg.array if isinstance(arg, Layer) else arg

    return pl.pallas_call(
        body,
        out_shape=[
            pltpu.HBM(shape, dtype) if pieces else jax.ShapeDtypeStruct(shape, dtype)
            for shape, dtype, pieces in all_outs
        ],
        in_specs=[space(isinstance(arg, (Far, Carry))) for arg in args],
        out_specs=[space(pieces > 0) for _, _, pieces in all_outs],
        scratch_shapes=scratch + [pltpu.SemaphoreType.DMA((max(semaphores, 1),))],
        compiler_params=pltpu.CompilerParams(vmem_limit_bytes=32 * 1024 * 1024),
    )(*[operand(arg) for arg in args])


def embed_kernel(x_ref, in_own, in_other, out_own, out_other, sender_w, slots, low_ref, high_ref,
                 proj_ref):
    x = x_ref[...]
    own = silu(matmul(in_own[...], x, 0)).astype(BF16)
    other = silu(matmul(in_other[...], x, 0)).astype(BF16)
    total = matmul(out_own[...], own, 0) + matmul(out_other[...], other, 0)
    latent = normalize(total, 0).astype(BF16)
    proj = matmul(sender_w[...], latent, 0).astype(BF16)
    proj_ref[...] = proj
    for block, out in ((0, low_ref), (2, high_ref)):
        pick = pick_columns(slots[block : block + 1, :], proj.shape[1])
        out[...] = matmul(proj, pick).astype(BF16)


def join(incoming, row, mesh_proj):
    pick = pick_columns(row, mesh_proj.shape[1])
    active = silu(incoming + matmul(mesh_proj, pick)).astype(BF16)
    return matmul(pick, jnp.transpose(active))


def prepare(latent, msg_own, msg_other, first_own, first_other, base_ref, fold_ref):
    width = latent.shape[1]
    firsts = (first_own, first_other)
    base_ref.put(0, jnp.concatenate([matmul(latent, each[:width, :]) for each in firsts], axis=1))
    fold = [
        jnp.concatenate([matmul(msg[...], each[width:, :]) for each in firsts], axis=1)
        for msg in (msg_own, msg_other)
    ]
    fold_ref.put(0, jnp.concatenate(fold, axis=0).astype(BF16))


def encode_mid_kernel(latent, receiver_w, grid_slots, mesh_slots, grid_proj, msg_own, msg_other,
                      first_own, first_other, proj_ref, sum_ref, base_ref, fold_ref):
    nodes = latent[...]
    proj = matmul(receiver_w[...], nodes, 0, 1).astype(BF16)
    proj_ref[...] = proj
    incoming = matmul(grid_proj[...], pick_columns(grid_slots[1:2, :], grid_proj.shape[1]))
    sum_ref[...] = join(incoming, mesh_slots[1:2, :], proj)
    prepare(nodes, msg_own, msg_other, first_own, first_other, base_ref, fold_ref)


def encode_far_kernel(mesh_proj, partial, mesh_slots, low, high, hidden_ref):
    proj = mesh_proj[...]
    total = partial[...] + join(low[...].astype(F32), mesh_slots[0:1, :], proj)
    total = total + join(high[...].astype(F32), mesh_slots[2:3, :], proj)
    hidden_ref[...] = total.astype(BF16)


def node_kernel(hidden_own, hidden_other, fold, base, second_own, second_other, latent, *refs):
    half = hidden_own.shape[1]
    pre_act = matmul(hidden_own[...], fold[:half, :]) + matmul(hidden_other[...], fold[half:, :])
    inner = silu(base[...] + pre_act).astype(BF16)
    total = matmul(inner[:, :half], second_own[...]) + matmul(inner[:, half:], second_other[...])
    new = (latent[...].astype(F32) + normalize(total, 1)).astype(BF16)
    if len(refs) == 1:
        refs[0][...] = new
        return
    sender_w, halo, new_ref, outgoing_ref = refs
    new_ref.put(0, new)
    local = matmul(new, sender_w[...]).astype(BF16)
    column = as_column(halo[...])
    rows = outgoing_ref.rows
    for start in range(0, column.shape[0], rows):
        picked = matmul(pick_rows(column[start : start + rows, :], local.shape[0]), local)
        outgoing_ref.put(start // rows, picked.astype(BF16))


def edge_near_kernel(latent, sender_w, receiver_w, edge_w, edges, senders, receivers, msg_own,
                     msg_other, first_own, first_other, near_ref, base_ref, fold_ref):
    nodes = latent[...]
    count = nodes.shape[0]
    table = [matmul(each[...], nodes, 0, 1).astype(BF16) for each in (sender_w, receiver_w)]
    table = jnp.concatenate(table, axis=1)
    rows = edges.rows
    for piece in range(edges.shape[0] // rows):
        place = slice(piece * rows, (piece + 1) * rows)
        pick = jnp.concatenate(
            [pick_columns(each[:, place], count) for each in (senders, receivers)], axis=0
        )
        near = matmul(edge_w[...], edges.piece(piece), 0, 1) + matmul(table, pick)
        near_ref.put(piece, near.astype(BF16))
    prepare(nodes, msg_own, msg_other, first_own, first_other, base_ref, fold_ref)


def edge_far_kernel(count, arrived, near, senders, receivers, hidden_ref):
    far = arrived.shape[0]
    table = jnp.transpose(arrived[...])
    rows = near.shape[1]
    total = None
    for piece in range(senders.shape[1] // rows):
        place = slice(piece * rows, (piece + 1) * rows)
        pre_act = matmul(table, pick_columns(senders[:, place] - count, far))
        pre_act = near.piece(piece).astype(F32) + pre_act
        pick = pick_columns(receivers[:, place], count)
        part = matmul(pick, jnp.transpose(silu(pre_act).astype(BF16)))
        total = part if total is None else total + part
    hidden_ref[...] = total.astype(BF16)


def swap(values):
    return lax.ppermute(values, "tp", [(0, 1), (1, 0)])


def shards(
    grid_input,
    mesh_latent,
    edge_latent,
    slot_grid_row,
    slot_mesh_row,
    halo_send,
    edge_sender,
    edge_receiver,
    embed_in,
    embed_out,
    encode_sender,
    encode_receiver,
    encode_out,
    encode_node_in,
    encode_node_out,
    layer_sender,
    layer_receiver,
    layer_edge,
    layer_message,
    layer_node_in,
    layer_node_out,
):
    nodes, width = mesh_latent.shape
    grid_rows = grid_input.shape[0]
    slot_count = slot_grid_row.shape[1]
    half = encode_sender.shape[1]
    bands, halo_slots = halo_send.shape
    layers = layer_sender.shape[0]
    pieces = 5
    edge_rows = edge_latent.shape[0] // pieces

    low, high, grid_proj = call(
        embed_kernel,
        [((half, slot_count), BF16, 0), ((half, slot_count), BF16, 0), ((half, grid_rows), BF16, 0)],
        grid_input.T, Far(embed_in), swap(embed_in), Far(embed_out), swap(embed_out),
        Far(encode_sender), slot_grid_row,
    )
    from_low = lax.ppermute(high, "band", [(i, i + 1) for i in range(bands - 1)])
    from_high = lax.ppermute(low, "band", [(i + 1, i) for i in range(bands - 1)])

    owned = (encode_out, encode_node_in, encode_node_out, layer_message, layer_node_in, layer_node_out)
    owned, grid_proj = lax.optimization_barrier((owned, grid_proj))
    encode_message, encode_first, encode_second, message, first, second = [
        (each, swap(each)) for each in owned
    ]

    def prepare_weights(message, first, layer):
        return [Far(each, layer) for pair in (message, first) for each in pair]

    prepared = [((nodes, width), F32, 1), ((width, width), BF16, 1)]
    mesh_proj, partial, base, fold = call(
        encode_mid_kernel, [((half, nodes), BF16, 0), ((nodes, half), F32, 0)] + prepared,
        Far(mesh_latent), Far(encode_receiver), slot_grid_row, slot_mesh_row, grid_proj,
        *prepare_weights(encode_message, encode_first, None),
    )
    hidden, *update, sender_w = call(
        encode_far_kernel, [((nodes, half), BF16, 0)], mesh_proj, partial, slot_mesh_row, from_low,
        from_high, Carry(fold), Carry(base), Carry(encode_second[0]), Carry(encode_second[1]),
        Carry(mesh_latent), Carry(layer_sender, 0),
    )

    halo_row = halo_send.reshape(1, -1)
    sender_row = edge_sender.reshape(1, -1)
    receiver_row = edge_receiver.reshape(1, -1)
    node_out = [((nodes, width), BF16, 1), ((bands * halo_slots, half), BF16, 4)]

    for layer in range(layers):
        latent, outgoing = call(
            node_kernel, node_out, hidden, swap(hidden), *update, sender_w, halo_row
        )
        arrived = lax.all_to_all(
            outgoing.reshape(bands, halo_slots, half), "band", split_axis=0, concat_axis=0, tiled=True
        ).reshape(bands * halo_slots, half)
        near, base, fold = call(
            edge_near_kernel, [((pieces * half, edge_rows), BF16, pieces)] + prepared, Far(latent),
            Far(layer_sender, layer), Far(layer_receiver, layer), Far(layer_edge, layer),
            Far(edge_latent, None, pieces), sender_row, receiver_row,
            *prepare_weights(message, first, layer),
        )
        (hidden,) = call(
            functools.partial(edge_far_kernel, nodes), [((nodes, half), BF16, 0)], arrived,
            Far(near, None, pieces), sender_row, receiver_row,
        )
        update = [fold, base, Layer(second[0], layer), Layer(second[1], layer), latent]
        if layer + 1 < layers:
            sender_w = Layer(layer_sender, layer + 1)
    (latent,) = call(node_kernel, [((nodes, width), BF16, 0)], hidden, swap(hidden), *update)
    return latent


def solution(mesh):
    return jax.shard_map(
        shards,
        mesh=mesh,
        in_specs=(
            P("band", None),
            P("band", None),
            P("band", None),
            P("band", None),
            P("band", None),
            P("band", None),
            P("band"),
            P("band"),
            P(None, "tp"),
            P("tp", None),
            P(None, "tp"),
            P(None, "tp"),
            P("tp", None),
            P(None, "tp"),
            P("tp", None),
            P(None, None, "tp"),
            P(None, None, "tp"),
            P(None, None, "tp"),
            P(None, "tp", None),
            P(None, None, "tp"),
            P(None, "tp", None),
        ),
        out_specs=P("band", None),
        check_vma=False,
    )
```

```python
import functools

import jax
import jax.numpy as jnp
from jax import lax
from jax.experimental import pallas as pl
from jax.experimental.pallas import tpu as pltpu
from jax.sharding import PartitionSpec as P

BF16 = jnp.bfloat16
F32 = jnp.float32


def matmul(left, right, left_dim=1, right_dim=0):
    dims = (((left_dim,), (right_dim,)), ((), ()))
    return lax.dot_general(left, right, dims, preferred_element_type=F32)


def silu(values):
    half = 0.5 * values
    return half + half * jnp.tanh(half)


def normalize(values, axis):
    centre = jnp.mean(values, axis=axis, keepdims=True)
    centered = values - centre
    variance = jnp.mean(centered * centered, axis=axis, keepdims=True)
    return centered * lax.rsqrt(variance + 1e-05)


def as_column(row):
    return jnp.transpose(jnp.broadcast_to(row, (128, row.shape[1])))


def pick_rows(column, count):
    n = column.shape[0]
    wide = jnp.concatenate([column] * pl.cdiv(count, 128), axis=1)[:, :count]
    lanes = lax.broadcasted_iota(jnp.int32, (n, count), 1)
    return jnp.where(wide == lanes, 1.0, 0.0).astype(BF16)


def pick_columns(row, count):
    n = row.shape[1]
    rows = lax.broadcasted_iota(jnp.int32, (count, n), 0)
    return jnp.where(row == rows, 1.0, 0.0).astype(BF16)


class Carry:
    def __init__(self, array, layer=None, used=False):
        self.array, self.layer, self.used, self.pieces = array, layer, used, 1
        self.shape = array.shape if layer is None else array.shape[1:]


class Layer:
    def __init__(self, array, layer):
        self.array, self.layer = array, layer


class Far:
    def __init__(self, array, layer=None, pieces=1):
        self.array, self.layer, self.pieces = array, layer, pieces
        self.shape = array.shape if layer is None else array.shape[1:]


class Incoming:
    def __init__(self, spec, ref, held, sems, first):
        source = ref if spec.layer is None else ref.at[spec.layer]
        self.held, self.shape, self.rows = held, spec.shape, spec.shape[0] // spec.pieces
        self.copies = []
        for piece in range(spec.pieces):
            rows = pl.ds(piece * self.rows, self.rows)
            self.copies.append(
                pltpu.make_async_copy(source.at[rows], held.at[rows], sems.at[first + piece])
            )
        self.waiting = [True] * spec.pieces
        for copy in self.copies:
            copy.start()

    def piece(self, index):
        if self.waiting[index]:
            self.copies[index].wait()
            self.waiting[index] = False
        return self.held[index * self.rows : (index + 1) * self.rows, :]

    def __getitem__(self, key):
        for index in range(len(self.copies)):
            self.piece(index)
        return self.held[key]


class Outgoing:
    def __init__(self, ref, held, sems, first, pieces):
        self.ref, self.held, self.sems, self.first = ref, held, sems, first
        self.rows, self.copies = ref.shape[0] // pieces, []

    def put(self, index, values):
        rows = pl.ds(index * self.rows, self.rows)
        self.held[index * self.rows : (index + 1) * self.rows, :] = values
        copy = pltpu.make_async_copy(
            self.held.at[rows], self.ref.at[rows], self.sems.at[self.first + index]
        )
        copy.start()
        self.copies.append(copy)


def call(kernel, outs, *args):
    scratch, semaphores = [], 0
    for arg in args:
        if isinstance(arg, Far):
            scratch.append(pltpu.VMEM(arg.shape, arg.array.dtype))
            semaphores += arg.pieces
    for shape, dtype, pieces in outs:
        if pieces:
            scratch.append(pltpu.VMEM(shape, dtype))
            semaphores += pieces
    carried = [arg for arg in args if isinstance(arg, Carry)]
    semaphores += len(carried)
    all_outs = list(outs) + [(arg.shape, arg.array.dtype, 0) for arg in carried]

    def body(*refs):
        inputs, refs = refs[: len(args)], refs[len(args) :]
        results, held = refs[: len(all_outs)], list(refs[len(all_outs) : -1])
        sems, first = refs[-1], 0
        copied = list(results[len(outs) :])
        taken, given, carries = [], [], []
        for arg, ref in zip(args, inputs):
            if isinstance(arg, Far):
                taken.append(Incoming(arg, ref, held.pop(0), sems, first))
                first += arg.pieces
            elif isinstance(arg, Carry):
                carries.append((arg, ref, copied.pop(0), first))
                if arg.used:
                    taken.append(Incoming(arg, ref, carries[-1][2], sems, first))
                first += 1
            else:
                taken.append(ref.at[arg.layer] if isinstance(arg, Layer) else ref)
        carries = [Incoming(*each[:3], sems, each[3]) for each in carries if not each[0].used]
        for (shape, dtype, pieces), ref in zip(outs, results):
            if pieces:
                ref = Outgoing(ref, held.pop(0), sems, first, pieces)
                first += pieces
            given.append(ref)
        kernel(*taken, *given)
        for ref in taken + carries:
            if isinstance(ref, Incoming):
                for index in range(len(ref.copies)):
                    if ref.waiting[index]:
                        ref.copies[index].wait()
        for ref in given:
            if isinstance(ref, Outgoing):
                for copy in ref.copies:
                    copy.wait()

    def space(far):
        return pl.BlockSpec(memory_space=pltpu.HBM if far else pltpu.VMEM)

    def operand(arg):
        if isinstance(arg, (Far, Carry)):
            return pltpu.with_memory_space_constraint(arg.array, pltpu.HBM)
        return arg.array if isinstance(arg, Layer) else arg

    return pl.pallas_call(
        body,
        out_shape=[
            pltpu.HBM(shape, dtype) if pieces else jax.ShapeDtypeStruct(shape, dtype)
            for shape, dtype, pieces in all_outs
        ],
        in_specs=[space(isinstance(arg, (Far, Carry))) for arg in args],
        out_specs=[space(pieces > 0) for _, _, pieces in all_outs],
        scratch_shapes=scratch + [pltpu.SemaphoreType.DMA((max(semaphores, 1),))],
        compiler_params=pltpu.CompilerParams(vmem_limit_bytes=32 * 1024 * 1024),
    )(*[operand(arg) for arg in args])


def embed_own_kernel(x, in_own, own_ref):
    own_ref[...] = silu(matmul(in_own[...], x[...], 0)).astype(BF16)


def embed_kernel(x, own, in_other, out_own, out_other, sender_own, sender_other, slots, send_ref,
                 proj_ref):
    other = silu(matmul(in_other[...], x[...], 0)).astype(BF16)
    total = matmul(out_own[...], own[...], 0) + matmul(out_other[...], other, 0)
    latent = normalize(total, 0).astype(BF16)
    proj = [matmul(each[...], latent, 0).astype(BF16) for each in (sender_own, sender_other)]
    proj = jnp.concatenate(proj, axis=0)
    proj_ref[...] = proj
    row = jnp.where(lax.axis_index("tp") == 0, slots[2:3, :], slots[0:1, :])
    send_ref[...] = matmul(proj, pick_columns(row, proj.shape[1])).astype(BF16)


def join(incoming, row, mesh_proj):
    pick = pick_columns(row, mesh_proj.shape[1])
    active = silu(incoming + matmul(mesh_proj, pick)).astype(BF16)
    return matmul(pick, jnp.transpose(active))


def prepare(latent, msg_own, msg_other, first_own, first_other, base_ref, fold_ref):
    width = latent.shape[1]
    firsts = (first_own, first_other)
    base_ref.put(0, jnp.concatenate([matmul(latent, each[:width, :]) for each in firsts], axis=1))
    fold = [
        jnp.concatenate([matmul(msg[...], each[width:, :]) for each in firsts], axis=1)
        for msg in (msg_own, msg_other)
    ]
    fold_ref.put(0, jnp.concatenate(fold, axis=0).astype(BF16))


def encode_mid_kernel(latent, receiver_own, receiver_other, grid_slots, mesh_slots, grid_proj,
                      msg_own, msg_other, first_own, first_other, proj_ref, sum_ref, base_ref,
                      fold_ref):
    nodes = latent[...]
    proj = [matmul(each[...], nodes, 0, 1).astype(BF16) for each in (receiver_own, receiver_other)]
    proj = jnp.concatenate(proj, axis=0)
    proj_ref[...] = proj
    half = grid_slots.shape[1] // 2
    low = lax.axis_index("tp") == 0
    grid_row, mesh_row = [
        jnp.where(low, each[1:2, :half], each[1:2, half:]) for each in (grid_slots, mesh_slots)
    ]
    incoming = matmul(grid_proj[...], pick_columns(grid_row, grid_proj.shape[1]))
    sum_ref[...] = join(incoming, mesh_row, proj)
    prepare(nodes, msg_own, msg_other, first_own, first_other, base_ref, fold_ref)


def encode_far_kernel(mesh_proj, partial, mesh_slots, arrived, sum_ref):
    row = jnp.where(lax.axis_index("tp") == 0, mesh_slots[0:1, :], mesh_slots[2:3, :])
    total = partial[...] + join(arrived[...].astype(F32), row, mesh_proj[...])
    sum_ref[...] = total.astype(BF16)


def node_kernel(hidden_own, hidden_other, fold, base, second_own, second_other, latent, *refs):
    half = second_own.shape[0]
    own, other = hidden_own[...], hidden_other[...]
    if own.shape[1] > half:
        mine, theirs = own.astype(F32), other.astype(F32)
        own = (mine[:, :half] + theirs[:, half:]).astype(BF16)
        other = (mine[:, half:] + theirs[:, :half]).astype(BF16)
    pre_act = matmul(own, fold[:half, :]) + matmul(other, fold[half:, :])
    inner = silu(base[...] + pre_act).astype(BF16)
    total = matmul(inner[:, :half], second_own[...]) + matmul(inner[:, half:], second_other[...])
    new = (latent[...].astype(F32) + normalize(total, 1)).astype(BF16)
    if len(refs) == 1:
        refs[0][...] = new
        return
    sender_w, halo, new_ref, outgoing_ref = refs
    new_ref.put(0, new)
    local = matmul(new, sender_w[...]).astype(BF16)
    column = as_column(halo[...])
    rows = outgoing_ref.rows
    for start in range(0, column.shape[0], rows):
        picked = matmul(pick_rows(column[start : start + rows, :], local.shape[0]), local)
        outgoing_ref.put(start // rows, picked.astype(BF16))


def edge_near_kernel(latent, sender_w, receiver_w, edge_w, edges, senders, receivers, msg_own,
                     msg_other, first_own, first_other, near_ref, base_ref, fold_ref):
    nodes = latent[...]
    count = nodes.shape[0]
    table = [matmul(each[...], nodes, 0, 1).astype(BF16) for each in (sender_w, receiver_w)]
    table = jnp.concatenate(table, axis=1)
    rows = edges.rows
    for piece in range(edges.shape[0] // rows):
        place = slice(piece * rows, (piece + 1) * rows)
        pick = jnp.concatenate(
            [pick_columns(each[:, place], count) for each in (senders, receivers)], axis=0
        )
        near = matmul(edge_w[...], edges.piece(piece), 0, 1) + matmul(table, pick)
        near_ref.put(piece, near.astype(BF16))
    prepare(nodes, msg_own, msg_other, first_own, first_other, base_ref, fold_ref)


def edge_far_kernel(count, arrived, near, senders, receivers, hidden_ref):
    far = arrived.shape[0]
    table = jnp.transpose(arrived[...])
    rows = near.shape[1]
    total = None
    for piece in range(senders.shape[1] // rows):
        place = slice(piece * rows, (piece + 1) * rows)
        pre_act = matmul(table, pick_columns(senders[:, place] - count, far))
        pre_act = near.piece(piece).astype(F32) + pre_act
        pick = pick_columns(receivers[:, place], count)
        part = matmul(pick, jnp.transpose(silu(pre_act).astype(BF16)))
        total = part if total is None else total + part
    hidden_ref[...] = total.astype(BF16)


def swap(values):
    return lax.ppermute(values, "tp", [(0, 1), (1, 0)])


def shards(
    grid_input,
    mesh_latent,
    edge_latent,
    slot_grid_row,
    slot_mesh_row,
    halo_send,
    edge_sender,
    edge_receiver,
    embed_in,
    embed_out,
    encode_sender,
    encode_receiver,
    encode_out,
    encode_node_in,
    encode_node_out,
    layer_sender,
    layer_receiver,
    layer_edge,
    layer_message,
    layer_node_in,
    layer_node_out,
):
    nodes, width = mesh_latent.shape
    grid_rows = grid_input.shape[0]
    slot_count = slot_grid_row.shape[1]
    half = encode_sender.shape[1]
    bands, halo_slots = halo_send.shape
    layers = layer_sender.shape[0]
    pieces = 5
    edge_rows = edge_latent.shape[0] // pieces

    own, x, out_own, sender_own = call(
        embed_own_kernel, [((half, grid_rows), BF16, 0)], Carry(grid_input.T, None, True),
        Far(embed_in), Carry(embed_out), Carry(encode_sender),
    )
    outgoing, grid_proj = call(
        embed_kernel, [((width, slot_count), BF16, 0), ((width, grid_rows), BF16, 0)], x, own,
        swap(embed_in), out_own, swap(embed_out), sender_own, swap(encode_sender),
        Far(slot_grid_row),
    )
    pairs = [(2 * i, 2 * i + 2) for i in range(bands - 1)]
    pairs += [(2 * i + 3, 2 * i + 1) for i in range(bands - 1)]
    arrived = lax.ppermute(outgoing, ("band", "tp"), pairs)

    owned = (encode_receiver, encode_out, encode_node_in, encode_node_out, layer_message,
             layer_node_in, layer_node_out)
    owned, grid_proj = lax.optimization_barrier((owned, grid_proj))
    receiver, encode_message, encode_first, encode_second, message, first, second = [
        (each, swap(each)) for each in owned
    ]

    def prepare_weights(message, first, layer):
        return [Far(each, layer) for pair in (message, first) for each in pair]

    prepared = [((nodes, width), F32, 1), ((width, width), BF16, 1)]
    mesh_proj, partial, base, fold = call(
        encode_mid_kernel, [((width, nodes), BF16, 0), ((nodes, width), F32, 0)] + prepared,
        Far(mesh_latent), Far(receiver[0]), Far(receiver[1]), Far(slot_grid_row),
        Far(slot_mesh_row), grid_proj, *prepare_weights(encode_message, encode_first, None),
    )
    hidden, *update, sender_w = call(
        encode_far_kernel, [((nodes, width), BF16, 0)], mesh_proj, partial, Far(slot_mesh_row),
        arrived, Carry(fold), Carry(base), Carry(encode_second[0]), Carry(encode_second[1]),
        Carry(mesh_latent), Carry(layer_sender, 0),
    )

    halo_row = halo_send.reshape(1, -1)
    sender_row = edge_sender.reshape(1, -1)
    receiver_row = edge_receiver.reshape(1, -1)
    node_out = [((nodes, width), BF16, 1), ((bands * halo_slots, half), BF16, 4)]

    for layer in range(layers):
        latent, outgoing = call(
            node_kernel, node_out, hidden, swap(hidden), *update, sender_w, halo_row
        )
        arrived = lax.all_to_all(
            outgoing.reshape(bands, halo_slots, half), "band", split_axis=0, concat_axis=0, tiled=True
        ).reshape(bands * halo_slots, half)
        near, base, fold = call(
            edge_near_kernel, [((pieces * half, edge_rows), BF16, pieces)] + prepared, Far(latent),
            Far(layer_sender, layer), Far(layer_receiver, layer), Far(layer_edge, layer),
            Far(edge_latent, None, pieces), sender_row, receiver_row,
            *prepare_weights(message, first, layer),
        )
        (hidden,) = call(
            functools.partial(edge_far_kernel, nodes), [((nodes, half), BF16, 0)], arrived,
            Far(near, None, pieces), sender_row, receiver_row,
        )
        update = [fold, base, Layer(second[0], layer), Layer(second[1], layer), latent]
        if layer + 1 < layers:
            sender_w = Layer(layer_sender, layer + 1)
    (latent,) = call(node_kernel, [((nodes, width), BF16, 0)], hidden, swap(hidden), *update)
    return latent


def solution(mesh):
    return jax.shard_map(
        shards,
        mesh=mesh,
        in_specs=(
            P("band", None),
            P("band", None),
            P("band", None),
            P("band", None),
            P("band", None),
            P("band", None),
            P("band"),
            P("band"),
            P(None, "tp"),
            P("tp", None),
            P(None, "tp"),
            P(None, "tp"),
            P("tp", None),
            P(None, "tp"),
            P("tp", None),
            P(None, None, "tp"),
            P(None, None, "tp"),
            P(None, None, "tp"),
            P(None, "tp", None),
            P(None, None, "tp"),
            P(None, "tp", None),
        ),
        out_specs=P("band", None),
        check_vma=False,
    )
```

```python
import functools

import jax
import jax.numpy as jnp
from jax import lax
from jax.experimental import pallas as pl
from jax.experimental.pallas import tpu as pltpu
from jax.sharding import PartitionSpec as P

BF16 = jnp.bfloat16
F32 = jnp.float32


def matmul(left, right, left_dim=1, right_dim=0):
    dims = (((left_dim,), (right_dim,)), ((), ()))
    return lax.dot_general(left, right, dims, preferred_element_type=F32)


def silu(values):
    half = 0.5 * values
    return half + half * jnp.tanh(half)


def normalize(values, axis):
    centre = jnp.mean(values, axis=axis, keepdims=True)
    centered = values - centre
    variance = jnp.mean(centered * centered, axis=axis, keepdims=True)
    return centered * lax.rsqrt(variance + 1e-05)


def as_column(row):
    return jnp.transpose(jnp.broadcast_to(row, (128, row.shape[1])))


def pick_rows(column, count):
    n = column.shape[0]
    wide = jnp.concatenate([column] * pl.cdiv(count, 128), axis=1)[:, :count]
    lanes = lax.broadcasted_iota(jnp.int32, (n, count), 1)
    return jnp.where(wide == lanes, 1.0, 0.0).astype(BF16)


def pick_columns(row, count):
    n = row.shape[1]
    rows = lax.broadcasted_iota(jnp.int32, (count, n), 0)
    return jnp.where(row == rows, 1.0, 0.0).astype(BF16)


class Carry:
    def __init__(self, array, layer=None, used=False):
        self.array, self.layer, self.used, self.pieces = array, layer, used, 1
        self.shape = array.shape if layer is None else array.shape[1:]


class Layer:
    def __init__(self, array, layer):
        self.array, self.layer = array, layer


class Far:
    def __init__(self, array, layer=None, pieces=1):
        self.array, self.layer, self.pieces = array, layer, pieces
        self.shape = array.shape if layer is None else array.shape[1:]


class Incoming:
    def __init__(self, spec, ref, held, sems, first):
        self.source = ref if spec.layer is None else ref.at[spec.layer]
        self.held, self.sems, self.first = held, sems, first
        self.shape, self.pieces, self.rows = spec.shape, spec.pieces, spec.shape[0] // spec.pieces
        self.waiting = True
        for index in range(self.pieces):
            self.copy(index).start()

    def copy(self, index):
        rows = pl.ds(index * self.rows, self.rows)
        sem = self.sems.at[self.first + index]
        return pltpu.make_async_copy(self.source.at[rows], self.held.at[rows], sem)

    def piece(self, index):
        self.waiting = False
        self.copy(index).wait()
        return self.held[pl.ds(pl.multiple_of(index * self.rows, self.rows), self.rows), :]

    def wait(self):
        if self.waiting:
            self.waiting = False
            for index in range(self.pieces):
                self.copy(index).wait()

    def __getitem__(self, key):
        self.wait()
        return self.held[key]


class Outgoing:
    def __init__(self, ref, held, sems, first, pieces):
        self.ref, self.held, self.sems, self.first = ref, held, sems, first
        self.pieces, self.rows = pieces, ref.shape[0] // pieces

    def copy(self, index):
        rows = pl.ds(index * self.rows, self.rows)
        sem = self.sems.at[self.first + index]
        return pltpu.make_async_copy(self.held.at[rows], self.ref.at[rows], sem)

    def put(self, index, values):
        self.held[pl.ds(pl.multiple_of(index * self.rows, self.rows), self.rows), :] = values
        self.copy(index).start()

    def wait(self):
        for index in range(self.pieces):
            self.copy(index).wait()


def call(kernel, outs, *args, extra=()):
    scratch, semaphores = [], 0
    for arg in args:
        if isinstance(arg, Far):
            scratch.append(pltpu.VMEM(arg.shape, arg.array.dtype))
            semaphores += arg.pieces
    for shape, dtype, pieces in outs:
        if pieces:
            scratch.append(pltpu.VMEM(shape, dtype))
            semaphores += pieces
    carried = [arg for arg in args if isinstance(arg, Carry)]
    semaphores += len(carried)
    all_outs = list(outs) + [(arg.shape, arg.array.dtype, 0) for arg in carried]

    def body(*refs):
        inputs, refs = refs[: len(args)], refs[len(args) :]
        results, held = refs[: len(all_outs)], list(refs[len(all_outs) : -1])
        held, own = held[: len(held) - len(extra)], held[len(held) - len(extra) :]
        sems, first = refs[-1], 0
        copied = list(results[len(outs) :])
        taken, given, carries = [], [], []
        for arg, ref in zip(args, inputs):
            if isinstance(arg, Far):
                taken.append(Incoming(arg, ref, held.pop(0), sems, first))
                first += arg.pieces
            elif isinstance(arg, Carry):
                carries.append((arg, ref, copied.pop(0), first))
                if arg.used:
                    taken.append(Incoming(arg, ref, carries[-1][2], sems, first))
                first += 1
            else:
                taken.append(ref.at[arg.layer] if isinstance(arg, Layer) else ref)
        carries = [Incoming(*each[:3], sems, each[3]) for each in carries if not each[0].used]
        for (shape, dtype, pieces), ref in zip(outs, results):
            if pieces:
                ref = Outgoing(ref, held.pop(0), sems, first, pieces)
                first += pieces
            given.append(ref)
        kernel(*taken, *given, *own)
        for ref in taken + carries + given:
            if isinstance(ref, (Incoming, Outgoing)):
                ref.wait()

    def space(far):
        return pl.BlockSpec(memory_space=pltpu.HBM if far else pltpu.VMEM)

    def operand(arg):
        if isinstance(arg, (Far, Carry)):
            return pltpu.with_memory_space_constraint(arg.array, pltpu.HBM)
        return arg.array if isinstance(arg, Layer) else arg

    return pl.pallas_call(
        body,
        out_shape=[
            pltpu.HBM(shape, dtype) if pieces else jax.ShapeDtypeStruct(shape, dtype)
            for shape, dtype, pieces in all_outs
        ],
        in_specs=[space(isinstance(arg, (Far, Carry))) for arg in args],
        out_specs=[space(pieces > 0) for _, _, pieces in all_outs],
        scratch_shapes=scratch + list(extra) + [pltpu.SemaphoreType.DMA((max(semaphores, 1),))],
        compiler_params=pltpu.CompilerParams(vmem_limit_bytes=32 * 1024 * 1024),
    )(*[operand(arg) for arg in args])


def each_block(count, block, body, init=None, unroll=1):
    def step(index, carry):
        return body(pl.ds(pl.multiple_of(index * block, block), block), index, carry)

    return lax.fori_loop(0, count // block, step, init, unroll=unroll)


def embed_own_kernel(block, x, in_own, own_ref):
    weight = in_own[...]
    x.wait()

    def step(columns, index, carry):
        own_ref[:, columns] = silu(matmul(weight, x[:, columns], 0)).astype(BF16)

    each_block(x.shape[1], block, step)


def embed_kernel(block, x, own, in_other, out_own, out_other, sender_own, sender_other, slots, send_ref,
                 proj_ref):
    half = sender_own.shape[1]

    def embed(columns, index, carry):
        other = silu(matmul(in_other[...], x[:, columns], 0)).astype(BF16)
        total = matmul(out_own[...], own[:, columns], 0) + matmul(out_other[...], other, 0)
        latent = normalize(total, 0).astype(BF16)
        proj_ref[:half, columns] = matmul(sender_own[...], latent, 0).astype(BF16)
        proj_ref[half:, columns] = matmul(sender_other[...], latent, 0).astype(BF16)

    each_block(x.shape[1], block, embed, unroll=True)
    slots.wait()

    def gather(columns, index, carry):
        low = lax.axis_index("tp") == 0
        row = jnp.where(low, slots[2:3, columns], slots[0:1, columns])
        pick = pick_columns(row, proj_ref.shape[1])
        send_ref[:, columns] = matmul(proj_ref[...], pick).astype(BF16)

    each_block(send_ref.shape[1], block, gather, unroll=True)


def join(incoming, row, mesh_proj):
    pick = pick_columns(row, mesh_proj.shape[1])
    active = silu(incoming + matmul(mesh_proj, pick)).astype(BF16)
    return matmul(pick, jnp.transpose(active))


def prepare(latent, msg_own, msg_other, first_own, first_other, base_ref, fold_ref):
    width = latent.shape[1]
    firsts = (first_own, first_other)
    base_ref.put(0, jnp.concatenate([matmul(latent, each[:width, :]) for each in firsts], axis=1))
    fold = [
        jnp.concatenate([matmul(msg[...], each[width:, :]) for each in firsts], axis=1)
        for msg in (msg_own, msg_other)
    ]
    fold_ref.put(0, jnp.concatenate(fold, axis=0).astype(BF16))


def encode_mid_kernel(block, latent, receiver_own, receiver_other, grid_slots, mesh_slots, grid_proj,
                      msg_own, msg_other, first_own, first_other, proj_ref, sum_ref, base_ref,
                      fold_ref):
    nodes = latent[...]
    half = receiver_own.shape[1]
    proj_ref[:half, :] = matmul(receiver_own[...], nodes, 0, 1).astype(BF16)
    proj_ref[half:, :] = matmul(receiver_other[...], nodes, 0, 1).astype(BF16)
    low = lax.axis_index("tp") == 0
    middle = grid_slots.shape[1] // 2
    grid_row, mesh_row = [
        jnp.where(low, each[1:2, :middle], each[1:2, middle:]) for each in (grid_slots, mesh_slots)
    ]
    incoming = matmul(grid_proj[...], pick_columns(grid_row, grid_proj.shape[1]))
    sum_ref[...] = join(incoming, mesh_row, proj_ref[...])
    prepare(nodes, msg_own, msg_other, first_own, first_other, base_ref, fold_ref)


def encode_far_kernel(block, mesh_proj, partial, mesh_slots, arrived, sum_ref, total_ref):
    total_ref[...] = partial[...]
    mesh_slots.wait()

    def step(columns, index, carry):
        low = lax.axis_index("tp") == 0
        row = jnp.where(low, mesh_slots[0:1, columns], mesh_slots[2:3, columns])
        total_ref[...] += join(arrived[:, columns].astype(F32), row, mesh_proj[...])

    each_block(arrived.shape[1], block, step, unroll=True)
    sum_ref[...] = total_ref[...].astype(BF16)


def node_kernel(hidden_own, hidden_other, fold, base, second_own, second_other, latent, *refs):
    half = second_own.shape[0]
    own, other = hidden_own[...], hidden_other[...]
    if own.shape[1] > half:
        mine, theirs = own.astype(F32), other.astype(F32)
        own = (mine[:, :half] + theirs[:, half:]).astype(BF16)
        other = (mine[:, half:] + theirs[:, :half]).astype(BF16)
    pre_act = matmul(own, fold[:half, :]) + matmul(other, fold[half:, :])
    inner = silu(base[...] + pre_act).astype(BF16)
    total = matmul(inner[:, :half], second_own[...]) + matmul(inner[:, half:], second_other[...])
    new = (latent[...].astype(F32) + normalize(total, 1)).astype(BF16)
    if len(refs) == 1:
        refs[0][...] = new
        return
    sender_w, halo, new_ref, outgoing_ref = refs
    new_ref.put(0, new)
    local = matmul(new, sender_w[...]).astype(BF16)

    def step(columns, index, carry):
        pick = pick_rows(as_column(halo[:, columns]), local.shape[0])
        outgoing_ref.put(index, matmul(pick, local).astype(BF16))

    each_block(halo.shape[1], outgoing_ref.rows, step, unroll=True)


def edge_near_kernel(latent, sender_w, receiver_w, edge_w, edges, senders, receivers, msg_own,
                     msg_other, first_own, first_other, near_ref, base_ref, fold_ref):
    nodes = latent[...]
    count = nodes.shape[0]
    table = [matmul(each[...], nodes, 0, 1).astype(BF16) for each in (sender_w, receiver_w)]
    table = jnp.concatenate(table, axis=1)
    weight = edge_w[...]

    def step(columns, index, carry):
        pick = jnp.concatenate(
            [pick_columns(each[:, columns], count) for each in (senders, receivers)], axis=0
        )
        near = matmul(weight, edges.piece(index), 0, 1) + matmul(table, pick)
        near_ref.put(index, near.astype(BF16))

    each_block(edges.shape[0], edges.rows, step)
    prepare(nodes, msg_own, msg_other, first_own, first_other, base_ref, fold_ref)


def edge_far_kernel(count, arrived, near, senders, receivers, hidden_ref):
    far = arrived.shape[0]
    table = jnp.transpose(arrived[...])

    def step(columns, index, total):
        pre_act = matmul(table, pick_columns(senders[:, columns] - count, far))
        pre_act = near.piece(index).astype(F32) + pre_act
        pick = pick_columns(receivers[:, columns], count)
        return total + matmul(pick, jnp.transpose(silu(pre_act).astype(BF16)))

    total = each_block(senders.shape[1], near.shape[1], step, jnp.zeros(hidden_ref.shape, F32))
    hidden_ref[...] = total.astype(BF16)


def swap(values):
    return lax.ppermute(values, "tp", [(0, 1), (1, 0)])


def shards(
    grid_input,
    mesh_latent,
    edge_latent,
    slot_grid_row,
    slot_mesh_row,
    halo_send,
    edge_sender,
    edge_receiver,
    embed_in,
    embed_out,
    encode_sender,
    encode_receiver,
    encode_out,
    encode_node_in,
    encode_node_out,
    layer_sender,
    layer_receiver,
    layer_edge,
    layer_message,
    layer_node_in,
    layer_node_out,
):
    nodes, width = mesh_latent.shape
    grid_rows = grid_input.shape[0]
    slot_count = slot_grid_row.shape[1]
    half = encode_sender.shape[1]
    bands, halo_slots = halo_send.shape
    layers = layer_sender.shape[0]
    pieces = 5
    block = 512
    edge_rows = edge_latent.shape[0] // pieces

    own, x, out_own, sender_own = call(
        functools.partial(embed_own_kernel, block), [((half, grid_rows), BF16, 0)], Carry(grid_input.T, None, True),
        Far(embed_in), Carry(embed_out), Carry(encode_sender),
    )
    outgoing, grid_proj = call(
        functools.partial(embed_kernel, block),
        [((width, slot_count), BF16, 0), ((width, grid_rows), BF16, 0)], x, own, swap(embed_in),
        out_own, swap(embed_out), sender_own, swap(encode_sender), Far(slot_grid_row),
    )
    pairs = [(2 * i, 2 * i + 2) for i in range(bands - 1)]
    pairs += [(2 * i + 3, 2 * i + 1) for i in range(bands - 1)]
    arrived = lax.ppermute(outgoing, ("band", "tp"), pairs)

    owned = (encode_receiver, encode_out, encode_node_in, encode_node_out, layer_message,
             layer_node_in, layer_node_out)
    owned, grid_proj = lax.optimization_barrier((owned, grid_proj))
    receiver, encode_message, encode_first, encode_second, message, first, second = [
        (each, swap(each)) for each in owned
    ]

    def prepare_weights(message, first, layer):
        return [Far(each, layer) for pair in (message, first) for each in pair]

    prepared = [((nodes, width), F32, 1), ((width, width), BF16, 1)]
    mesh_proj, partial, base, fold = call(
        functools.partial(encode_mid_kernel, block),
        [((width, nodes), BF16, 0), ((nodes, width), F32, 0)] + prepared,
        Far(mesh_latent), Far(receiver[0]), Far(receiver[1]), Far(slot_grid_row),
        Far(slot_mesh_row), grid_proj, *prepare_weights(encode_message, encode_first, None),
    )
    hidden, *update, sender_w = call(
        functools.partial(encode_far_kernel, block), [((nodes, width), BF16, 0)], mesh_proj,
        partial, Far(slot_mesh_row), arrived, Carry(fold), Carry(base), Carry(encode_second[0]),
        Carry(encode_second[1]), Carry(mesh_latent), Carry(layer_sender, 0),
        extra=[pltpu.VMEM((nodes, width), F32)],
    )

    halo_row = halo_send.reshape(1, -1)
    sender_row = edge_sender.reshape(1, -1)
    receiver_row = edge_receiver.reshape(1, -1)
    node_out = [((nodes, width), BF16, 1), ((bands * halo_slots, half), BF16, 4)]

    for layer in range(layers):
        latent, outgoing = call(
            node_kernel, node_out, hidden, swap(hidden), *update, sender_w, halo_row
        )
        arrived = lax.all_to_all(
            outgoing.reshape(bands, halo_slots, half), "band", split_axis=0, concat_axis=0, tiled=True
        ).reshape(bands * halo_slots, half)
        near, base, fold = call(
            edge_near_kernel, [((pieces * half, edge_rows), BF16, pieces)] + prepared, Far(latent),
            Far(layer_sender, layer), Far(layer_receiver, layer), Far(layer_edge, layer),
            Far(edge_latent, None, pieces), sender_row, receiver_row,
            *prepare_weights(message, first, layer),
        )
        (hidden,) = call(
            functools.partial(edge_far_kernel, nodes), [((nodes, half), BF16, 0)], arrived,
            Far(near, None, pieces), sender_row, receiver_row,
        )
        update = [fold, base, Layer(second[0], layer), Layer(second[1], layer), latent]
        if layer + 1 < layers:
            sender_w = Layer(layer_sender, layer + 1)
    (latent,) = call(node_kernel, [((nodes, width), BF16, 0)], hidden, swap(hidden), *update)
    return latent


def solution(mesh):
    return jax.shard_map(
        shards,
        mesh=mesh,
        in_specs=(
            P("band", None),
            P("band", None),
            P("band", None),
            P("band", None),
            P("band", None),
            P("band", None),
            P("band"),
            P("band"),
            P(None, "tp"),
            P("tp", None),
            P(None, "tp"),
            P(None, "tp"),
            P("tp", None),
            P(None, "tp"),
            P("tp", None),
            P(None, None, "tp"),
            P(None, None, "tp"),
            P(None, None, "tp"),
            P(None, "tp", None),
            P(None, None, "tp"),
            P(None, "tp", None),
        ),
        out_specs=P("band", None),
        check_vma=False,
    )
```

```python
import functools

import jax
import jax.numpy as jnp
import numpy as np
from jax import lax
from jax.experimental import pallas as pl
from jax.experimental.pallas import tpu as pltpu
from jax.sharding import PartitionSpec as P

BF16 = jnp.bfloat16
F32 = jnp.float32


def matmul(left, right, left_dim=1, right_dim=0):
    dims = (((left_dim,), (right_dim,)), ((), ()))
    return lax.dot_general(left, right, dims, preferred_element_type=F32)


def silu(values):
    half = 0.5 * values
    return half + half * jnp.tanh(half)


def normalize(values, axis):
    centre = jnp.mean(values, axis=axis, keepdims=True)
    centered = values - centre
    variance = jnp.mean(centered * centered, axis=axis, keepdims=True)
    return centered * lax.rsqrt(variance + 1e-05)


def as_column(row):
    return jnp.transpose(jnp.broadcast_to(row, (128, row.shape[1])))


def pick_rows(column, count):
    n = column.shape[0]
    wide = jnp.concatenate([column] * pl.cdiv(count, 128), axis=1)[:, :count]
    lanes = lax.broadcasted_iota(jnp.int32, (n, count), 1)
    return jnp.where(wide == lanes, 1.0, 0.0).astype(BF16)


def pick_columns(row, count):
    n = row.shape[1]
    rows = lax.broadcasted_iota(jnp.int32, (count, n), 0)
    return jnp.where(row == rows, 1.0, 0.0).astype(BF16)


class Carry:
    def __init__(self, array, layer=None, used=False):
        self.array, self.layer, self.used, self.pieces = array, layer, used, 1
        self.shape = array.shape if layer is None else array.shape[1:]


class Layer:
    def __init__(self, array, layer):
        self.array, self.layer = array, layer


class Far:
    def __init__(self, array, layer=None, pieces=1):
        self.array, self.layer, self.pieces = array, layer, pieces
        self.shape = array.shape if layer is None else array.shape[1:]


class Incoming:
    def __init__(self, spec, ref, held, sems, first):
        self.source = ref if spec.layer is None else ref.at[spec.layer]
        self.held, self.sems, self.first = held, sems, first
        self.shape, self.pieces, self.rows = spec.shape, spec.pieces, spec.shape[0] // spec.pieces
        self.waiting = True
        for index in range(self.pieces):
            self.copy(index).start()

    def copy(self, index):
        rows = pl.ds(index * self.rows, self.rows)
        sem = self.sems.at[self.first + index]
        return pltpu.make_async_copy(self.source.at[rows], self.held.at[rows], sem)

    def piece(self, index):
        self.waiting = False
        self.copy(index).wait()
        return self.held[pl.ds(pl.multiple_of(index * self.rows, self.rows), self.rows), :]

    def wait(self):
        if self.waiting:
            self.waiting = False
            for index in range(self.pieces):
                self.copy(index).wait()

    def __getitem__(self, key):
        self.wait()
        return self.held[key]


class Outgoing:
    def __init__(self, ref, held, sems, first, pieces):
        self.ref, self.held, self.sems, self.first = ref, held, sems, first
        self.pieces, self.rows = pieces, ref.shape[0] // pieces

    def copy(self, index):
        rows = pl.ds(index * self.rows, self.rows)
        sem = self.sems.at[self.first + index]
        return pltpu.make_async_copy(self.held.at[rows], self.ref.at[rows], sem)

    def put(self, index, values):
        self.held[pl.ds(pl.multiple_of(index * self.rows, self.rows), self.rows), :] = values
        self.copy(index).start()

    def wait(self):
        for index in range(self.pieces):
            self.copy(index).wait()


def call(kernel, outs, *args, extra=()):
    scratch, semaphores = [], 0
    for arg in args:
        if isinstance(arg, Far):
            scratch.append(pltpu.VMEM(arg.shape, arg.array.dtype))
            semaphores += arg.pieces
    for shape, dtype, pieces in outs:
        if pieces:
            scratch.append(pltpu.VMEM(shape, dtype))
            semaphores += pieces
    carried = [arg for arg in args if isinstance(arg, Carry)]
    semaphores += len(carried)
    all_outs = list(outs) + [(arg.shape, arg.array.dtype, 0) for arg in carried]

    def body(*refs):
        inputs, refs = refs[: len(args)], refs[len(args) :]
        results, held = refs[: len(all_outs)], list(refs[len(all_outs) : -1])
        held, own = held[: len(held) - len(extra)], held[len(held) - len(extra) :]
        sems, first = refs[-1], 0
        copied = list(results[len(outs) :])
        taken, given, carries = [], [], []
        for arg, ref in zip(args, inputs):
            if isinstance(arg, Far):
                taken.append(Incoming(arg, ref, held.pop(0), sems, first))
                first += arg.pieces
            elif isinstance(arg, Carry):
                carries.append((arg, ref, copied.pop(0), first))
                if arg.used:
                    taken.append(Incoming(arg, ref, carries[-1][2], sems, first))
                first += 1
            else:
                taken.append(ref.at[arg.layer] if isinstance(arg, Layer) else ref)
        carries = [Incoming(*each[:3], sems, each[3]) for each in carries if not each[0].used]
        for (shape, dtype, pieces), ref in zip(outs, results):
            if pieces:
                ref = Outgoing(ref, held.pop(0), sems, first, pieces)
                first += pieces
            given.append(ref)
        kernel(*taken, *given, *own)
        for ref in taken + carries + given:
            if isinstance(ref, (Incoming, Outgoing)):
                ref.wait()

    def space(far):
        return pl.BlockSpec(memory_space=pltpu.HBM if far else pltpu.VMEM)

    def operand(arg):
        if isinstance(arg, (Far, Carry)):
            return pltpu.with_memory_space_constraint(arg.array, pltpu.HBM)
        return arg.array if isinstance(arg, Layer) else arg

    return pl.pallas_call(
        body,
        out_shape=[
            pltpu.HBM(shape, dtype) if pieces else jax.ShapeDtypeStruct(shape, dtype)
            for shape, dtype, pieces in all_outs
        ],
        in_specs=[space(isinstance(arg, (Far, Carry))) for arg in args],
        out_specs=[space(pieces > 0) for _, _, pieces in all_outs],
        scratch_shapes=scratch + list(extra) + [pltpu.SemaphoreType.DMA((max(semaphores, 1),))],
        compiler_params=pltpu.CompilerParams(vmem_limit_bytes=32 * 1024 * 1024),
    )(*[operand(arg) for arg in args])


def each_block(count, block, body, init=None, unroll=1):
    def step(index, carry):
        return body(pl.ds(pl.multiple_of(index * block, block), block), index, carry)

    return lax.fori_loop(0, count // block, step, init, unroll=unroll)


def embed_own_kernel(block, x, in_own, own_ref):
    weight = in_own[...]
    x.wait()

    def step(columns, index, carry):
        own_ref[:, columns] = silu(matmul(weight, x[:, columns], 0)).astype(BF16)

    each_block(x.shape[1], block, step)


def embed_kernel(block, x, own, in_other, out_own, out_other, sender_own, sender_other, slots, send_ref,
                 proj_ref):
    half = sender_own.shape[1]

    def embed(columns, index, carry):
        other = silu(matmul(in_other[...], x[:, columns], 0)).astype(BF16)
        total = matmul(out_own[...], own[:, columns], 0) + matmul(out_other[...], other, 0)
        latent = normalize(total, 0).astype(BF16)
        proj_ref[:half, columns] = matmul(sender_own[...], latent, 0).astype(BF16)
        proj_ref[half:, columns] = matmul(sender_other[...], latent, 0).astype(BF16)

    each_block(x.shape[1], block, embed, unroll=True)
    slots.wait()

    def gather(columns, index, carry):
        low = lax.axis_index("tp") == 0
        row = jnp.where(low, slots[2:3, columns], slots[0:1, columns])
        pick = pick_columns(row, proj_ref.shape[1])
        send_ref[:, columns] = matmul(proj_ref[...], pick).astype(BF16)

    each_block(send_ref.shape[1], block, gather, unroll=True)


def join(incoming, row, mesh_proj):
    pick = pick_columns(row, mesh_proj.shape[1])
    active = silu(incoming + matmul(mesh_proj, pick)).astype(BF16)
    return matmul(pick, jnp.transpose(active))


def prepare(latent, msg_own, msg_other, first_own, first_other, base_ref, fold_ref):
    width = latent.shape[1]
    firsts = (first_own, first_other)
    base_ref.put(0, jnp.concatenate([matmul(latent, each[:width, :]) for each in firsts], axis=1))
    fold = [
        jnp.concatenate([matmul(msg[...], each[width:, :]) for each in firsts], axis=1)
        for msg in (msg_own, msg_other)
    ]
    fold_ref.put(0, jnp.concatenate(fold, axis=0).astype(BF16))


def encode_mid_kernel(block, latent, receiver_own, receiver_other, grid_slots, mesh_slots, grid_proj,
                      msg_own, msg_other, first_own, first_other, proj_ref, sum_ref, base_ref,
                      fold_ref):
    nodes = latent[...]
    half = receiver_own.shape[1]
    proj_ref[:half, :] = matmul(receiver_own[...], nodes, 0, 1).astype(BF16)
    proj_ref[half:, :] = matmul(receiver_other[...], nodes, 0, 1).astype(BF16)
    low = lax.axis_index("tp") == 0
    middle = grid_slots.shape[1] // 2
    grid_row, mesh_row = [
        jnp.where(low, each[1:2, :middle], each[1:2, middle:]) for each in (grid_slots, mesh_slots)
    ]
    incoming = matmul(grid_proj[...], pick_columns(grid_row, grid_proj.shape[1]))
    sum_ref[...] = join(incoming, mesh_row, proj_ref[...])
    prepare(nodes, msg_own, msg_other, first_own, first_other, base_ref, fold_ref)


def encode_far_kernel(block, mesh_proj, partial, mesh_slots, arrived, sum_ref, total_ref):
    total_ref[...] = partial[...]
    mesh_slots.wait()

    def step(columns, index, carry):
        low = lax.axis_index("tp") == 0
        row = jnp.where(low, mesh_slots[0:1, columns], mesh_slots[2:3, columns])
        total_ref[...] += join(arrived[:, columns].astype(F32), row, mesh_proj[...])

    each_block(arrived.shape[1], block, step, unroll=True)
    sum_ref[...] = total_ref[...].astype(BF16)


def node_kernel(hidden_own, hidden_other, fold, base, second_own, second_other, latent, *refs):
    half = second_own.shape[0]
    own, other = hidden_own[...], hidden_other[...]
    if own.shape[1] > half:
        mine, theirs = own.astype(F32), other.astype(F32)
        own = (mine[:, :half] + theirs[:, half:]).astype(BF16)
        other = (mine[:, half:] + theirs[:, :half]).astype(BF16)
    pre_act = matmul(own, fold[:half, :]) + matmul(other, fold[half:, :])
    inner = silu(base[...] + pre_act).astype(BF16)
    total = matmul(inner[:, :half], second_own[...]) + matmul(inner[:, half:], second_other[...])
    new = (latent[...].astype(F32) + normalize(total, 1)).astype(BF16)
    if len(refs) == 1:
        refs[0][...] = new
        return
    sender_w, halo, new_ref, outgoing_ref = refs
    new_ref.put(0, new)
    local = matmul(new, sender_w[...]).astype(BF16)

    def step(columns, index, carry):
        pick = pick_rows(as_column(halo[:, columns]), local.shape[0])
        outgoing_ref.put(index, matmul(pick, local).astype(BF16))

    each_block(halo.shape[1], outgoing_ref.rows, step, unroll=True)


def edge_near_kernel(latent, sender_w, receiver_w, edge_w, edges, senders, receivers, msg_own,
                     msg_other, first_own, first_other, near_ref, base_ref, fold_ref):
    nodes = latent[...]
    count = nodes.shape[0]
    table = [matmul(each[...], nodes, 0, 1).astype(BF16) for each in (sender_w, receiver_w)]
    table = jnp.concatenate(table, axis=1)
    weight = edge_w[...]

    def step(columns, index, carry):
        pick = jnp.concatenate(
            [pick_columns(each[:, columns], count) for each in (senders, receivers)], axis=0
        )
        near = matmul(weight, edges.piece(index), 0, 1) + matmul(table, pick)
        near_ref.put(index, near.astype(BF16))

    each_block(edges.shape[0], edges.rows, step)
    prepare(nodes, msg_own, msg_other, first_own, first_other, base_ref, fold_ref)


def edge_far_kernel(count, arrived, near, senders, receivers, hidden_ref):
    far = arrived.shape[0]
    table = jnp.transpose(arrived[...])

    def step(columns, index, total):
        pre_act = matmul(table, pick_columns(senders[:, columns] - count, far))
        pre_act = near.piece(index).astype(F32) + pre_act
        pick = pick_columns(receivers[:, columns], count)
        return total + matmul(pick, jnp.transpose(silu(pre_act).astype(BF16)))

    total = each_block(senders.shape[1], near.shape[1], step, jnp.zeros(hidden_ref.shape, F32))
    hidden_ref[...] = total.astype(BF16)


def swap(values):
    return lax.ppermute(values, "tp", [(0, 1), (1, 0)])


def shards(
    grid_input,
    mesh_latent,
    edge_latent,
    slot_grid_row,
    slot_mesh_row,
    halo_send,
    edge_sender,
    edge_receiver,
    embed_in,
    embed_out,
    encode_sender,
    encode_receiver,
    encode_out,
    encode_node_in,
    encode_node_out,
    layer_sender,
    layer_receiver,
    layer_edge,
    layer_message,
    layer_node_in,
    layer_node_out,
):
    nodes, width = mesh_latent.shape
    grid_rows = grid_input.shape[0]
    slot_count = slot_grid_row.shape[1]
    half = encode_sender.shape[1]
    bands, halo_slots = halo_send.shape
    layers = layer_sender.shape[0]
    pieces = 5
    block = 512
    edge_rows = edge_latent.shape[0] // pieces

    own, x, out_own, sender_own = call(
        functools.partial(embed_own_kernel, block), [((half, grid_rows), BF16, 0)], Carry(grid_input.T, None, True),
        Far(embed_in), Carry(embed_out), Carry(encode_sender),
    )
    outgoing, grid_proj = call(
        functools.partial(embed_kernel, block),
        [((width, slot_count), BF16, 0), ((width, grid_rows), BF16, 0)], x, own, swap(embed_in),
        out_own, swap(embed_out), sender_own, swap(encode_sender), Far(slot_grid_row),
    )
    pairs = [(2 * i, 2 * i + 2) for i in range(bands - 1)]
    pairs += [(2 * i + 3, 2 * i + 1) for i in range(bands - 1)]
    arrived = lax.ppermute(outgoing, ("band", "tp"), pairs)

    owned = (encode_receiver, encode_out, encode_node_in, encode_node_out, layer_message,
             layer_node_in, layer_node_out)
    owned, grid_proj = lax.optimization_barrier((owned, grid_proj))
    receiver, encode_message, encode_first, encode_second, message, first, second = [
        (each, swap(each)) for each in owned
    ]

    def prepare_weights(message, first, layer):
        return [Far(each, layer) for pair in (message, first) for each in pair]

    prepared = [((nodes, width), F32, 1), ((width, width), BF16, 1)]
    mesh_proj, partial, base, fold = call(
        functools.partial(encode_mid_kernel, block),
        [((width, nodes), BF16, 0), ((nodes, width), F32, 0)] + prepared,
        Far(mesh_latent), Far(receiver[0]), Far(receiver[1]), Far(slot_grid_row),
        Far(slot_mesh_row), grid_proj, *prepare_weights(encode_message, encode_first, None),
    )
    hidden, *update, sender_w = call(
        functools.partial(encode_far_kernel, block), [((nodes, width), BF16, 0)], mesh_proj,
        partial, Far(slot_mesh_row), arrived, Carry(fold), Carry(base), Carry(encode_second[0]),
        Carry(encode_second[1]), Carry(mesh_latent), Carry(layer_sender, 0),
        extra=[pltpu.VMEM((nodes, width), F32)],
    )

    order = (6, 5, 4, 3, 2, 1, 0)
    bits = len(order)
    members = np.arange(bands).reshape((2,) * bits).transpose(order).reshape(-1).tolist()
    halo_row = halo_send.reshape((2,) * bits + (halo_slots,)).transpose(order + (bits,)).reshape(1, -1)
    slot = edge_sender - nodes
    place = slot & (halo_slots - 1)
    for to, bit in enumerate(order):
        place += ((slot // (halo_slots << (bits - 1 - bit))) & 1) * (halo_slots << (bits - 1 - to))
    sender_row = jnp.where(slot < 0, edge_sender, place + nodes).reshape(1, -1)
    receiver_row = edge_receiver.reshape(1, -1)
    node_out = [((nodes, width), BF16, 1), ((bands * halo_slots, half), BF16, 4)]

    for layer in range(layers):
        latent, outgoing = call(
            node_kernel, node_out, hidden, swap(hidden), *update, sender_w, halo_row
        )
        arrived = lax.all_to_all(
            outgoing.reshape(bands, halo_slots, half), "band", split_axis=0, concat_axis=0,
            axis_index_groups=[members], tiled=True
        ).reshape(bands * halo_slots, half)
        near, base, fold = call(
            edge_near_kernel, [((pieces * half, edge_rows), BF16, pieces)] + prepared, Far(latent),
            Far(layer_sender, layer), Far(layer_receiver, layer), Far(layer_edge, layer),
            Far(edge_latent, None, pieces), sender_row, receiver_row,
            *prepare_weights(message, first, layer),
        )
        (hidden,) = call(
            functools.partial(edge_far_kernel, nodes), [((nodes, half), BF16, 0)], arrived,
            Far(near, None, pieces), sender_row, receiver_row,
        )
        update = [fold, base, Layer(second[0], layer), Layer(second[1], layer), latent]
        if layer + 1 < layers:
            sender_w = Layer(layer_sender, layer + 1)
    (latent,) = call(node_kernel, [((nodes, width), BF16, 0)], hidden, swap(hidden), *update)
    return latent


def solution(mesh):
    return jax.shard_map(
        shards,
        mesh=mesh,
        in_specs=(
            P("band", None),
            P("band", None),
            P("band", None),
            P("band", None),
            P("band", None),
            P("band", None),
            P("band"),
            P("band"),
            P(None, "tp"),
            P("tp", None),
            P(None, "tp"),
            P(None, "tp"),
            P("tp", None),
            P(None, "tp"),
            P("tp", None),
            P(None, None, "tp"),
            P(None, None, "tp"),
            P(None, None, "tp"),
            P(None, "tp", None),
            P(None, None, "tp"),
            P(None, "tp", None),
        ),
        out_specs=P("band", None),
        check_vma=False,
    )
```

```python
import functools

import jax
import jax.numpy as jnp
import numpy as np
from jax import lax
from jax.experimental import pallas as pl
from jax.experimental.pallas import tpu as pltpu
from jax.sharding import PartitionSpec as P

BF16 = jnp.bfloat16
F32 = jnp.float32


def matmul(left, right, left_dim=1, right_dim=0):
    dims = (((left_dim,), (right_dim,)), ((), ()))
    return lax.dot_general(left, right, dims, preferred_element_type=F32)


def silu(values):
    half = 0.5 * values
    return half + half * jnp.tanh(half)


def normalize(values, axis):
    centre = jnp.mean(values, axis=axis, keepdims=True)
    centered = values - centre
    variance = jnp.mean(centered * centered, axis=axis, keepdims=True)
    return centered * lax.rsqrt(variance + 1e-05)


def as_column(row):
    return jnp.transpose(jnp.broadcast_to(row, (128, row.shape[1])))


def pick_rows(column, count):
    n = column.shape[0]
    wide = jnp.concatenate([column] * pl.cdiv(count, 128), axis=1)[:, :count]
    lanes = lax.broadcasted_iota(jnp.int32, (n, count), 1)
    return jnp.where(wide == lanes, 1.0, 0.0).astype(BF16)


def pick_columns(row, count):
    n = row.shape[1]
    rows = lax.broadcasted_iota(jnp.int32, (count, n), 0)
    return jnp.where(row == rows, 1.0, 0.0).astype(BF16)


class Carry:
    def __init__(self, array, layer=None, used=False):
        self.array, self.layer, self.used, self.pieces = array, layer, used, 1
        self.shape = array.shape if layer is None else array.shape[1:]


class Layer:
    def __init__(self, array, layer):
        self.array, self.layer = array, layer


class Far:
    def __init__(self, array, layer=None, pieces=1):
        self.array, self.layer, self.pieces = array, layer, pieces
        self.shape = array.shape if layer is None else array.shape[1:]


class Incoming:
    def __init__(self, spec, ref, held, sems, first):
        self.source = ref if spec.layer is None else ref.at[spec.layer]
        self.held, self.sems, self.first = held, sems, first
        self.shape, self.pieces, self.rows = spec.shape, spec.pieces, spec.shape[0] // spec.pieces
        self.waiting = True
        for index in range(self.pieces):
            self.copy(index).start()

    def copy(self, index):
        rows = pl.ds(index * self.rows, self.rows)
        sem = self.sems.at[self.first + index]
        return pltpu.make_async_copy(self.source.at[rows], self.held.at[rows], sem)

    def piece(self, index):
        self.waiting = False
        self.copy(index).wait()
        return self.held[pl.ds(pl.multiple_of(index * self.rows, self.rows), self.rows), :]

    def wait(self):
        if self.waiting:
            self.waiting = False
            for index in range(self.pieces):
                self.copy(index).wait()

    def __getitem__(self, key):
        self.wait()
        return self.held[key]


class Outgoing:
    def __init__(self, ref, held, sems, first, pieces):
        self.ref, self.held, self.sems, self.first = ref, held, sems, first
        self.pieces, self.rows = pieces, ref.shape[0] // pieces

    def copy(self, index):
        rows = pl.ds(index * self.rows, self.rows)
        sem = self.sems.at[self.first + index]
        return pltpu.make_async_copy(self.held.at[rows], self.ref.at[rows], sem)

    def put(self, index, values):
        self.held[pl.ds(pl.multiple_of(index * self.rows, self.rows), self.rows), :] = values
        self.copy(index).start()

    def wait(self):
        for index in range(self.pieces):
            self.copy(index).wait()


def call(kernel, outs, *args, extra=()):
    scratch, semaphores = [], 0
    for arg in args:
        if isinstance(arg, Far):
            scratch.append(pltpu.VMEM(arg.shape, arg.array.dtype))
            semaphores += arg.pieces
    for shape, dtype, pieces in outs:
        if pieces:
            scratch.append(pltpu.VMEM(shape, dtype))
            semaphores += pieces
    carried = [arg for arg in args if isinstance(arg, Carry)]
    semaphores += len(carried)
    all_outs = list(outs) + [(arg.shape, arg.array.dtype, 0) for arg in carried]

    def body(*refs):
        inputs, refs = refs[: len(args)], refs[len(args) :]
        results, held = refs[: len(all_outs)], list(refs[len(all_outs) : -1])
        held, own = held[: len(held) - len(extra)], held[len(held) - len(extra) :]
        sems, first = refs[-1], 0
        copied = list(results[len(outs) :])
        taken, given, carries = [], [], []
        for arg, ref in zip(args, inputs):
            if isinstance(arg, Far):
                taken.append(Incoming(arg, ref, held.pop(0), sems, first))
                first += arg.pieces
            elif isinstance(arg, Carry):
                carries.append((arg, ref, copied.pop(0), first))
                if arg.used:
                    taken.append(Incoming(arg, ref, carries[-1][2], sems, first))
                first += 1
            else:
                taken.append(ref.at[arg.layer] if isinstance(arg, Layer) else ref)
        carries = [Incoming(*each[:3], sems, each[3]) for each in carries if not each[0].used]
        for (shape, dtype, pieces), ref in zip(outs, results):
            if pieces:
                ref = Outgoing(ref, held.pop(0), sems, first, pieces)
                first += pieces
            given.append(ref)
        kernel(*taken, *given, *own)
        for ref in taken + carries + given:
            if isinstance(ref, (Incoming, Outgoing)):
                ref.wait()

    def space(far):
        return pl.BlockSpec(memory_space=pltpu.HBM if far else pltpu.VMEM)

    def operand(arg):
        if isinstance(arg, (Far, Carry)):
            return pltpu.with_memory_space_constraint(arg.array, pltpu.HBM)
        return arg.array if isinstance(arg, Layer) else arg

    return pl.pallas_call(
        body,
        out_shape=[
            pltpu.HBM(shape, dtype) if pieces else jax.ShapeDtypeStruct(shape, dtype)
            for shape, dtype, pieces in all_outs
        ],
        in_specs=[space(isinstance(arg, (Far, Carry))) for arg in args],
        out_specs=[space(pieces > 0) for _, _, pieces in all_outs],
        scratch_shapes=scratch + list(extra) + [pltpu.SemaphoreType.DMA((max(semaphores, 1),))],
        compiler_params=pltpu.CompilerParams(vmem_limit_bytes=32 * 1024 * 1024),
    )(*[operand(arg) for arg in args])


def each_block(count, block, body, init=None, unroll=1):
    def step(index, carry):
        return body(pl.ds(pl.multiple_of(index * block, block), block), index, carry)

    return lax.fori_loop(0, count // block, step, init, unroll=unroll)


def embed_own_kernel(block, x, in_own, own_ref):
    weight = in_own[...]
    x.wait()

    def step(columns, index, carry):
        own_ref[:, columns] = silu(matmul(weight, x[:, columns], 0)).astype(BF16)

    each_block(x.shape[1], block, step)


def embed_kernel(block, x, own, in_other, out_own, out_other, sender_own, sender_other, slots, send_ref,
                 proj_ref):
    half = sender_own.shape[1]

    def embed(columns, index, carry):
        other = silu(matmul(in_other[...], x[:, columns], 0)).astype(BF16)
        total = matmul(out_own[...], own[:, columns], 0) + matmul(out_other[...], other, 0)
        latent = normalize(total, 0).astype(BF16)
        proj_ref[:half, columns] = matmul(sender_own[...], latent, 0).astype(BF16)
        proj_ref[half:, columns] = matmul(sender_other[...], latent, 0).astype(BF16)

    each_block(x.shape[1], block, embed, unroll=True)
    slots.wait()

    def gather(columns, index, carry):
        low = lax.axis_index("tp") == 0
        row = jnp.where(low, slots[2:3, columns], slots[0:1, columns])
        pick = pick_columns(row, proj_ref.shape[1])
        send_ref[:, columns] = matmul(proj_ref[...], pick).astype(BF16)

    each_block(send_ref.shape[1], block, gather, unroll=True)


def join(incoming, row, mesh_proj):
    pick = pick_columns(row, mesh_proj.shape[1])
    active = silu(incoming + matmul(mesh_proj, pick)).astype(BF16)
    return matmul(pick, jnp.transpose(active))


def prepare(latent, msg_own, msg_other, first_own, first_other, base_ref, fold_ref):
    width = latent.shape[1]
    firsts = (first_own, first_other)
    base_ref.put(0, jnp.concatenate([matmul(latent, each[:width, :]) for each in firsts], axis=1))
    fold = [
        jnp.concatenate([matmul(msg[...], each[width:, :]) for each in firsts], axis=1)
        for msg in (msg_own, msg_other)
    ]
    fold_ref.put(0, jnp.concatenate(fold, axis=0).astype(BF16))


def encode_mid_kernel(block, latent, receiver_own, receiver_other, grid_slots, mesh_slots, grid_proj,
                      msg_own, msg_other, first_own, first_other, proj_ref, sum_ref, base_ref,
                      fold_ref):
    nodes = latent[...]
    half = receiver_own.shape[1]
    proj_ref[:half, :] = matmul(receiver_own[...], nodes, 0, 1).astype(BF16)
    proj_ref[half:, :] = matmul(receiver_other[...], nodes, 0, 1).astype(BF16)
    low = lax.axis_index("tp") == 0
    middle = grid_slots.shape[1] // 2
    grid_row, mesh_row = [
        jnp.where(low, each[1:2, :middle], each[1:2, middle:]) for each in (grid_slots, mesh_slots)
    ]
    incoming = matmul(grid_proj[...], pick_columns(grid_row, grid_proj.shape[1]))
    sum_ref[...] = join(incoming, mesh_row, proj_ref[...])
    prepare(nodes, msg_own, msg_other, first_own, first_other, base_ref, fold_ref)


def encode_far_kernel(block, mesh_proj, partial, mesh_slots, arrived, sum_ref, total_ref):
    total_ref[...] = partial[...]
    mesh_slots.wait()

    def step(columns, index, carry):
        low = lax.axis_index("tp") == 0
        row = jnp.where(low, mesh_slots[0:1, columns], mesh_slots[2:3, columns])
        total_ref[...] += join(arrived[:, columns].astype(F32), row, mesh_proj[...])

    each_block(arrived.shape[1], block, step, unroll=True)
    sum_ref[...] = total_ref[...].astype(BF16)


def node_kernel(hidden_own, hidden_other, fold, base, second_own, second_other, latent, *refs):
    half = second_own.shape[0]
    own, other = hidden_own[...], hidden_other[...]
    if own.shape[1] > half:
        mine, theirs = own.astype(F32), other.astype(F32)
        own = (mine[:, :half] + theirs[:, half:]).astype(BF16)
        other = (mine[:, half:] + theirs[:, :half]).astype(BF16)
    pre_act = matmul(own, fold[:half, :]) + matmul(other, fold[half:, :])
    inner = silu(base[...] + pre_act).astype(BF16)
    total = matmul(inner[:, :half], second_own[...]) + matmul(inner[:, half:], second_other[...])
    new = (latent[...].astype(F32) + normalize(total, 1)).astype(BF16)
    if len(refs) == 1:
        refs[0][...] = new
        return
    sender_w, halo, new_ref, outgoing_ref = refs
    new_ref.put(0, new)
    local = matmul(new, sender_w[...]).astype(BF16)

    def step(columns, index, carry):
        pick = pick_rows(as_column(halo[:, columns]), local.shape[0])
        outgoing_ref.put(index, matmul(pick, local).astype(BF16))

    each_block(halo.shape[1], outgoing_ref.rows, step, unroll=True)


def edge_near_kernel(latent, sender_w, receiver_w, edge_w, edges, senders, receivers, msg_own,
                     msg_other, first_own, first_other, near_ref, base_ref, fold_ref):
    nodes = latent[...]
    count = nodes.shape[0]
    table = [matmul(each[...], nodes, 0, 1).astype(BF16) for each in (sender_w, receiver_w)]
    table = jnp.concatenate(table, axis=1)
    weight = edge_w[...]

    def step(columns, index, carry):
        pick = jnp.concatenate(
            [pick_columns(each[:, columns], count) for each in (senders, receivers)], axis=0
        )
        near = matmul(weight, edges.piece(index), 0, 1) + matmul(table, pick)
        near_ref.put(index, near.astype(BF16))

    each_block(edges.shape[0], edges.rows, step)
    prepare(nodes, msg_own, msg_other, first_own, first_other, base_ref, fold_ref)


def edge_far_kernel(count, arrived, near, senders, receivers, hidden_ref):
    far = arrived.shape[0]
    table = jnp.transpose(arrived[...])

    def step(columns, index, total):
        pre_act = matmul(table, pick_columns(senders[:, columns] - count, far))
        pre_act = near.piece(index).astype(F32) + pre_act
        pick = pick_columns(receivers[:, columns], count)
        return total + matmul(pick, jnp.transpose(silu(pre_act).astype(BF16)))

    total = each_block(senders.shape[1], near.shape[1], step, jnp.zeros(hidden_ref.shape, F32))
    hidden_ref[...] = total.astype(BF16)


def swap(values):
    return lax.ppermute(values, "tp", [(0, 1), (1, 0)])


def shards(
    grid_input,
    mesh_latent,
    edge_latent,
    slot_grid_row,
    slot_mesh_row,
    halo_send,
    edge_sender,
    edge_receiver,
    embed_in,
    embed_out,
    encode_sender,
    encode_receiver,
    encode_out,
    encode_node_in,
    encode_node_out,
    layer_sender,
    layer_receiver,
    layer_edge,
    layer_message,
    layer_node_in,
    layer_node_out,
):
    nodes, width = mesh_latent.shape
    grid_rows = grid_input.shape[0]
    slot_count = slot_grid_row.shape[1]
    half = encode_sender.shape[1]
    bands, halo_slots = halo_send.shape
    layers = layer_sender.shape[0]
    pieces = 1
    block = 1024
    edge_rows = edge_latent.shape[0] // pieces

    own, x, out_own, sender_own = call(
        functools.partial(embed_own_kernel, block), [((half, grid_rows), BF16, 0)], Carry(grid_input.T, None, True),
        Far(embed_in), Carry(embed_out), Carry(encode_sender),
    )
    outgoing, grid_proj = call(
        functools.partial(embed_kernel, block),
        [((width, slot_count), BF16, 0), ((width, grid_rows), BF16, 0)], x, own, swap(embed_in),
        out_own, swap(embed_out), sender_own, swap(encode_sender), Far(slot_grid_row),
    )
    pairs = [(2 * i, 2 * i + 2) for i in range(bands - 1)]
    pairs += [(2 * i + 3, 2 * i + 1) for i in range(bands - 1)]
    arrived = lax.ppermute(outgoing, ("band", "tp"), pairs)

    owned = (encode_receiver, encode_out, encode_node_in, encode_node_out, layer_message,
             layer_node_in, layer_node_out)
    owned, grid_proj = lax.optimization_barrier((owned, grid_proj))
    receiver, encode_message, encode_first, encode_second, message, first, second = [
        (each, swap(each)) for each in owned
    ]

    def prepare_weights(message, first, layer):
        return [Far(each, layer) for pair in (message, first) for each in pair]

    prepared = [((nodes, width), F32, 1), ((width, width), BF16, 1)]
    mesh_proj, partial, base, fold = call(
        functools.partial(encode_mid_kernel, block),
        [((width, nodes), BF16, 0), ((nodes, width), F32, 0)] + prepared,
        Far(mesh_latent), Far(receiver[0]), Far(receiver[1]), Far(slot_grid_row),
        Far(slot_mesh_row), grid_proj, *prepare_weights(encode_message, encode_first, None),
    )
    hidden, *update, sender_w = call(
        functools.partial(encode_far_kernel, block), [((nodes, width), BF16, 0)], mesh_proj,
        partial, Far(slot_mesh_row), arrived, Carry(fold), Carry(base), Carry(encode_second[0]),
        Carry(encode_second[1]), Carry(mesh_latent), Carry(layer_sender, 0),
        extra=[pltpu.VMEM((nodes, width), F32)],
    )

    order = (6, 5, 4, 3, 2, 1, 0)
    bits = len(order)
    members = np.arange(bands).reshape((2,) * bits).transpose(order).reshape(-1).tolist()
    halo_row = halo_send.reshape((2,) * bits + (halo_slots,)).transpose(order + (bits,)).reshape(1, -1)
    slot = edge_sender - nodes
    place = slot & (halo_slots - 1)
    for to, bit in enumerate(order):
        place += ((slot // (halo_slots << (bits - 1 - bit))) & 1) * (halo_slots << (bits - 1 - to))
    sender_row = jnp.where(slot < 0, edge_sender, place + nodes).reshape(1, -1)
    receiver_row = edge_receiver.reshape(1, -1)
    node_out = [((nodes, width), BF16, 1), ((bands * halo_slots, half), BF16, 4)]

    for layer in range(layers):
        latent, outgoing = call(
            node_kernel, node_out, hidden, swap(hidden), *update, sender_w, halo_row
        )
        arrived = lax.all_to_all(
            outgoing.reshape(bands, halo_slots, half), "band", split_axis=0, concat_axis=0,
            axis_index_groups=[members], tiled=True
        ).reshape(bands * halo_slots, half)
        near, base, fold = call(
            edge_near_kernel, [((pieces * half, edge_rows), BF16, pieces)] + prepared, Far(latent),
            Far(layer_sender, layer), Far(layer_receiver, layer), Far(layer_edge, layer),
            Far(edge_latent, None, pieces), sender_row, receiver_row,
            *prepare_weights(message, first, layer),
        )
        (hidden,) = call(
            functools.partial(edge_far_kernel, nodes), [((nodes, half), BF16, 0)], arrived,
            Far(near, None, pieces), sender_row, receiver_row,
        )
        update = [fold, base, Layer(second[0], layer), Layer(second[1], layer), latent]
        if layer + 1 < layers:
            sender_w = Layer(layer_sender, layer + 1)
    (latent,) = call(node_kernel, [((nodes, width), BF16, 0)], hidden, swap(hidden), *update)
    return latent


def solution(mesh):
    return jax.shard_map(
        shards,
        mesh=mesh,
        in_specs=(
            P("band", None),
            P("band", None),
            P("band", None),
            P("band", None),
            P("band", None),
            P("band", None),
            P("band"),
            P("band"),
            P(None, "tp"),
            P("tp", None),
            P(None, "tp"),
            P(None, "tp"),
            P("tp", None),
            P(None, "tp"),
            P("tp", None),
            P(None, None, "tp"),
            P(None, None, "tp"),
            P(None, None, "tp"),
            P(None, "tp", None),
            P(None, None, "tp"),
            P(None, "tp", None),
        ),
        out_specs=P("band", None),
        check_vma=False,
    )
```

```python
import functools

import jax
import jax.numpy as jnp
import numpy as np
from jax import lax
from jax.experimental import pallas as pl
from jax.experimental.pallas import tpu as pltpu
from jax.sharding import PartitionSpec as P

BF16 = jnp.bfloat16
F32 = jnp.float32


def matmul(left, right, left_dim=1, right_dim=0):
    dims = (((left_dim,), (right_dim,)), ((), ()))
    return lax.dot_general(left, right, dims, preferred_element_type=F32)


def silu(values):
    half = 0.5 * values
    return half + half * jnp.tanh(half)


def normalize(values, axis):
    centre = jnp.mean(values, axis=axis, keepdims=True)
    centered = values - centre
    variance = jnp.mean(centered * centered, axis=axis, keepdims=True)
    return centered * lax.rsqrt(variance + 1e-05)


def as_column(row):
    return jnp.transpose(jnp.broadcast_to(row, (128, row.shape[1])))


def pick_rows(column, count):
    n = column.shape[0]
    wide = jnp.concatenate([column] * pl.cdiv(count, 128), axis=1)[:, :count]
    lanes = lax.broadcasted_iota(jnp.int32, (n, count), 1)
    return jnp.where(wide == lanes, 1.0, 0.0).astype(BF16)


def pick_columns(row, count):
    n = row.shape[1]
    rows = lax.broadcasted_iota(jnp.int32, (count, n), 0)
    return jnp.where(row == rows, 1.0, 0.0).astype(BF16)


class Carry:
    def __init__(self, array, layer=None, used=False):
        self.array, self.layer, self.used, self.pieces = array, layer, used, 1
        self.shape = array.shape if layer is None else array.shape[1:]


class Layer:
    def __init__(self, array, layer):
        self.array, self.layer = array, layer


class Far:
    def __init__(self, array, layer=None, pieces=1):
        self.array, self.layer, self.pieces = array, layer, pieces
        self.shape = array.shape if layer is None else array.shape[1:]


class Incoming:
    def __init__(self, spec, ref, held, sems, first):
        self.source = ref if spec.layer is None else ref.at[spec.layer]
        self.held, self.sems, self.first = held, sems, first
        self.shape, self.pieces, self.rows = spec.shape, spec.pieces, spec.shape[0] // spec.pieces
        self.waiting = True
        for index in range(self.pieces):
            self.copy(index).start()

    def copy(self, index):
        rows = pl.ds(index * self.rows, self.rows)
        sem = self.sems.at[self.first + index]
        return pltpu.make_async_copy(self.source.at[rows], self.held.at[rows], sem)

    def piece(self, index):
        self.waiting = False
        self.copy(index).wait()
        return self.held[pl.ds(pl.multiple_of(index * self.rows, self.rows), self.rows), :]

    def wait(self):
        if self.waiting:
            self.waiting = False
            for index in range(self.pieces):
                self.copy(index).wait()

    def __getitem__(self, key):
        self.wait()
        return self.held[key]


class Outgoing:
    def __init__(self, ref, held, sems, first, pieces):
        self.ref, self.held, self.sems, self.first = ref, held, sems, first
        self.pieces, self.rows = pieces, ref.shape[0] // pieces

    def copy(self, index):
        rows = pl.ds(index * self.rows, self.rows)
        sem = self.sems.at[self.first + index]
        return pltpu.make_async_copy(self.held.at[rows], self.ref.at[rows], sem)

    def put(self, index, values):
        self.held[pl.ds(pl.multiple_of(index * self.rows, self.rows), self.rows), :] = values
        self.copy(index).start()

    def wait(self):
        for index in range(self.pieces):
            self.copy(index).wait()


def call(kernel, outs, *args, extra=()):
    scratch, semaphores = [], 0
    for arg in args:
        if isinstance(arg, Far):
            scratch.append(pltpu.VMEM(arg.shape, arg.array.dtype))
            semaphores += arg.pieces
    for shape, dtype, pieces in outs:
        if pieces:
            scratch.append(pltpu.VMEM(shape, dtype))
            semaphores += pieces
    carried = [arg for arg in args if isinstance(arg, Carry)]
    semaphores += len(carried)
    all_outs = list(outs) + [(arg.shape, arg.array.dtype, 0) for arg in carried]

    def body(*refs):
        inputs, refs = refs[: len(args)], refs[len(args) :]
        results, held = refs[: len(all_outs)], list(refs[len(all_outs) : -1])
        held, own = held[: len(held) - len(extra)], held[len(held) - len(extra) :]
        sems, first = refs[-1], 0
        copied = list(results[len(outs) :])
        taken, given, carries = [], [], []
        for arg, ref in zip(args, inputs):
            if isinstance(arg, Far):
                taken.append(Incoming(arg, ref, held.pop(0), sems, first))
                first += arg.pieces
            elif isinstance(arg, Carry):
                carries.append((arg, ref, copied.pop(0), first))
                if arg.used:
                    taken.append(Incoming(arg, ref, carries[-1][2], sems, first))
                first += 1
            else:
                taken.append(ref.at[arg.layer] if isinstance(arg, Layer) else ref)
        carries = [Incoming(*each[:3], sems, each[3]) for each in carries if not each[0].used]
        for (shape, dtype, pieces), ref in zip(outs, results):
            if pieces:
                ref = Outgoing(ref, held.pop(0), sems, first, pieces)
                first += pieces
            given.append(ref)
        kernel(*taken, *given, *own)
        for ref in taken + carries + given:
            if isinstance(ref, (Incoming, Outgoing)):
                ref.wait()

    def space(far):
        return pl.BlockSpec(memory_space=pltpu.HBM if far else pltpu.VMEM)

    def operand(arg):
        if isinstance(arg, (Far, Carry)):
            return pltpu.with_memory_space_constraint(arg.array, pltpu.HBM)
        return arg.array if isinstance(arg, Layer) else arg

    return pl.pallas_call(
        body,
        out_shape=[
            pltpu.HBM(shape, dtype) if pieces else jax.ShapeDtypeStruct(shape, dtype)
            for shape, dtype, pieces in all_outs
        ],
        in_specs=[space(isinstance(arg, (Far, Carry))) for arg in args],
        out_specs=[space(pieces > 0) for _, _, pieces in all_outs],
        scratch_shapes=scratch + list(extra) + [pltpu.SemaphoreType.DMA((max(semaphores, 1),))],
        compiler_params=pltpu.CompilerParams(vmem_limit_bytes=32 * 1024 * 1024),
    )(*[operand(arg) for arg in args])


def each_block(count, block, body, init=None, unroll=1):
    def step(index, carry):
        return body(pl.ds(pl.multiple_of(index * block, block), block), index, carry)

    return lax.fori_loop(0, count // block, step, init, unroll=unroll)


def embed_own_kernel(block, x, in_own, own_ref):
    weight = in_own[...]
    x.wait()

    def step(columns, index, carry):
        own_ref[:, columns] = silu(matmul(weight, x[:, columns], 0)).astype(BF16)

    each_block(x.shape[1], block, step)


def embed_kernel(block, x, own, in_other, out_own, out_other, sender_own, sender_other, slots, send_ref,
                 proj_ref):
    half = sender_own.shape[1]

    def embed(columns, index, carry):
        other = silu(matmul(in_other[...], x[:, columns], 0)).astype(BF16)
        total = matmul(out_own[...], own[:, columns], 0) + matmul(out_other[...], other, 0)
        latent = normalize(total, 0).astype(BF16)
        proj_ref[:half, columns] = matmul(sender_own[...], latent, 0).astype(BF16)
        proj_ref[half:, columns] = matmul(sender_other[...], latent, 0).astype(BF16)

    each_block(x.shape[1], block, embed, unroll=True)
    slots.wait()

    def gather(columns, index, carry):
        low = lax.axis_index("tp") == 0
        row = jnp.where(low, slots[2:3, columns], slots[0:1, columns])
        pick = pick_columns(row, proj_ref.shape[1])
        send_ref[:, columns] = matmul(proj_ref[...], pick).astype(BF16)

    each_block(send_ref.shape[1], block, gather, unroll=True)


def join(incoming, row, mesh_proj):
    pick = pick_columns(row, mesh_proj.shape[1])
    active = silu(incoming + matmul(mesh_proj, pick)).astype(BF16)
    return matmul(pick, jnp.transpose(active))


def prepare(latent, msg_own, msg_other, first_own, first_other, base_ref, fold_ref):
    width = latent.shape[1]
    firsts = (first_own, first_other)
    base = jnp.concatenate([matmul(latent, each[:width, :]) for each in firsts], axis=1)
    fold = [
        jnp.concatenate([matmul(msg[...], each[width:, :]) for each in firsts], axis=1)
        for msg in (msg_own, msg_other)
    ]
    fold = jnp.concatenate(fold, axis=0).astype(BF16)
    for values, ref in ((base, base_ref), (fold, fold_ref)):
        if isinstance(ref, Outgoing):
            ref.put(0, values)
        else:
            ref[...] = values


def encode_mid_kernel(latent, receiver_own, receiver_other, grid_slots, mesh_slots, grid_proj,
                      msg_own, msg_other, first_own, first_other, gathered_ref, pick_ref,
                      sum_ref, base_ref, fold_ref, proj_ref):
    nodes = latent[...]
    half = receiver_own.shape[1]
    proj_ref[:half, :] = matmul(receiver_own[...], nodes, 0, 1).astype(BF16)
    proj_ref[half:, :] = matmul(receiver_other[...], nodes, 0, 1).astype(BF16)
    low = lax.axis_index("tp") == 0
    middle = grid_slots.shape[1] // 2
    grid_row, mesh_row = [
        jnp.where(low, each[1:2, :middle], each[1:2, middle:]) for each in (grid_slots, mesh_slots)
    ]
    incoming = matmul(grid_proj[...], pick_columns(grid_row, grid_proj.shape[1]))
    sum_ref[...] = join(incoming, mesh_row, proj_ref[...])
    pick = pick_columns(jnp.where(low, mesh_slots[0:1, :], mesh_slots[2:3, :]), nodes.shape[0])
    pick_ref[...] = pick
    gathered_ref[...] = matmul(proj_ref[...], pick).astype(BF16)
    prepare(nodes, msg_own, msg_other, first_own, first_other, base_ref, fold_ref)


def encode_far_kernel(gathered, pick, partial, arrived, sum_ref):
    active = silu(arrived[...].astype(F32) + gathered[...].astype(F32)).astype(BF16)
    sum_ref[...] = (partial[...] + matmul(pick[...], jnp.transpose(active))).astype(BF16)


def node_kernel(hidden_own, hidden_other, fold, base, second_own, second_other, latent, *refs):
    half = second_own.shape[0]
    own, other = hidden_own[...], hidden_other[...]
    if own.shape[1] > half:
        mine, theirs = own.astype(F32), other.astype(F32)
        own = (mine[:, :half] + theirs[:, half:]).astype(BF16)
        other = (mine[:, half:] + theirs[:, :half]).astype(BF16)
    pre_act = matmul(own, fold[:half, :]) + matmul(other, fold[half:, :])
    inner = silu(base[...] + pre_act).astype(BF16)
    total = matmul(inner[:, :half], second_own[...]) + matmul(inner[:, half:], second_other[...])
    new = (latent[...].astype(F32) + normalize(total, 1)).astype(BF16)
    if len(refs) == 1:
        refs[0][...] = new
        return
    sender_w, halo, new_ref, outgoing_ref = refs
    new_ref.put(0, new)
    local = matmul(new, sender_w[...]).astype(BF16)

    def step(columns, index, carry):
        pick = pick_rows(as_column(halo[:, columns]), local.shape[0])
        outgoing_ref.put(index, matmul(pick, local).astype(BF16))

    each_block(halo.shape[1], outgoing_ref.rows, step, unroll=True)


def edge_near_kernel(latent, sender_w, receiver_w, edge_w, edges, senders, receivers, msg_own,
                     msg_other, first_own, first_other, near_ref, base_ref, fold_ref):
    nodes = latent[...]
    count = nodes.shape[0]
    table = [matmul(each[...], nodes, 0, 1).astype(BF16) for each in (sender_w, receiver_w)]
    table = jnp.concatenate(table, axis=1)
    weight = edge_w[...]

    def step(columns, index, carry):
        pick = jnp.concatenate(
            [pick_columns(each[:, columns], count) for each in (senders, receivers)], axis=0
        )
        near = matmul(weight, edges.piece(index), 0, 1) + matmul(table, pick)
        near_ref.put(index, near.astype(BF16))

    each_block(edges.shape[0], edges.rows, step)
    prepare(nodes, msg_own, msg_other, first_own, first_other, base_ref, fold_ref)


def edge_far_kernel(count, arrived, near, senders, receivers, hidden_ref):
    far = arrived.shape[0]
    table = jnp.transpose(arrived[...])

    def step(columns, index, total):
        pre_act = matmul(table, pick_columns(senders[:, columns] - count, far))
        pre_act = near.piece(index).astype(F32) + pre_act
        pick = pick_columns(receivers[:, columns], count)
        return total + matmul(pick, jnp.transpose(silu(pre_act).astype(BF16)))

    total = each_block(senders.shape[1], near.shape[1], step, jnp.zeros(hidden_ref.shape, F32))
    hidden_ref[...] = total.astype(BF16)


def swap(values):
    return lax.ppermute(values, "tp", [(0, 1), (1, 0)])


def shards(
    grid_input,
    mesh_latent,
    edge_latent,
    slot_grid_row,
    slot_mesh_row,
    halo_send,
    edge_sender,
    edge_receiver,
    embed_in,
    embed_out,
    encode_sender,
    encode_receiver,
    encode_out,
    encode_node_in,
    encode_node_out,
    layer_sender,
    layer_receiver,
    layer_edge,
    layer_message,
    layer_node_in,
    layer_node_out,
):
    nodes, width = mesh_latent.shape
    grid_rows = grid_input.shape[0]
    slot_count = slot_grid_row.shape[1]
    half = encode_sender.shape[1]
    bands, halo_slots = halo_send.shape
    layers = layer_sender.shape[0]
    pieces = 1
    block = 1024
    edge_rows = edge_latent.shape[0] // pieces

    own, x, out_own, sender_own = call(
        functools.partial(embed_own_kernel, block), [((half, grid_rows), BF16, 0)], Carry(grid_input.T, None, True),
        Far(embed_in), Carry(embed_out), Carry(encode_sender),
    )
    outgoing, grid_proj = call(
        functools.partial(embed_kernel, block),
        [((width, slot_count), BF16, 0), ((width, grid_rows), BF16, 0)], x, own, swap(embed_in),
        out_own, swap(embed_out), sender_own, swap(encode_sender), Far(slot_grid_row),
    )
    pairs = [(2 * i, 2 * i + 2) for i in range(bands - 1)]
    pairs += [(2 * i + 3, 2 * i + 1) for i in range(bands - 1)]
    arrived = lax.ppermute(outgoing, ("band", "tp"), pairs)

    owned = (encode_receiver, encode_out, encode_node_in, encode_node_out, layer_message,
             layer_node_in, layer_node_out)
    owned, grid_proj = lax.optimization_barrier((owned, grid_proj))
    receiver, encode_message, encode_first, encode_second, message, first, second = [
        (each, swap(each)) for each in owned
    ]

    def prepare_weights(message, first, layer):
        return [Far(each, layer) for pair in (message, first) for each in pair]

    prepared = [((nodes, width), F32, 1), ((width, width), BF16, 1)]
    gathered, pick, partial, base, fold, *update, sender_w = call(
        encode_mid_kernel,
        [((width, slot_count), BF16, 0), ((nodes, slot_count), BF16, 0), ((nodes, width), F32, 0),
         ((nodes, width), F32, 0), ((width, width), BF16, 0)],
        Far(mesh_latent), Far(receiver[0]), Far(receiver[1]), Far(slot_grid_row),
        Far(slot_mesh_row), grid_proj, *prepare_weights(encode_message, encode_first, None),
        Carry(encode_second[0]), Carry(encode_second[1]), Carry(mesh_latent),
        Carry(layer_sender, 0), extra=[pltpu.VMEM((width, nodes), BF16)],
    )
    (hidden,) = call(
        encode_far_kernel, [((nodes, width), BF16, 0)], gathered, pick, partial, arrived,
    )

    order = (6, 5, 4, 3, 2, 1, 0)
    bits = len(order)
    members = np.arange(bands).reshape((2,) * bits).transpose(order).reshape(-1).tolist()
    halo_row = halo_send.reshape((2,) * bits + (halo_slots,)).transpose(order + (bits,)).reshape(1, -1)
    slot = edge_sender - nodes
    place = slot & (halo_slots - 1)
    for to, bit in enumerate(order):
        place += ((slot // (halo_slots << (bits - 1 - bit))) & 1) * (halo_slots << (bits - 1 - to))
    sender_row = jnp.where(slot < 0, edge_sender, place + nodes).reshape(1, -1)
    receiver_row = edge_receiver.reshape(1, -1)
    update = [fold, base, *update]
    node_out = [((nodes, width), BF16, 1), ((bands * halo_slots, half), BF16, 4)]

    for layer in range(layers):
        latent, outgoing = call(
            node_kernel, node_out, hidden, swap(hidden), *update, sender_w, halo_row
        )
        arrived = lax.all_to_all(
            outgoing.reshape(bands, halo_slots, half), "band", split_axis=0, concat_axis=0,
            axis_index_groups=[members], tiled=True
        ).reshape(bands * halo_slots, half)
        near, base, fold = call(
            edge_near_kernel, [((pieces * half, edge_rows), BF16, pieces)] + prepared, Far(latent),
            Far(layer_sender, layer), Far(layer_receiver, layer), Far(layer_edge, layer),
            Far(edge_latent, None, pieces), sender_row, receiver_row,
            *prepare_weights(message, first, layer),
        )
        (hidden,) = call(
            functools.partial(edge_far_kernel, nodes), [((nodes, half), BF16, 0)], arrived,
            Far(near, None, pieces), sender_row, receiver_row,
        )
        update = [fold, base, Layer(second[0], layer), Layer(second[1], layer), latent]
        if layer + 1 < layers:
            sender_w = Layer(layer_sender, layer + 1)
    (latent,) = call(node_kernel, [((nodes, width), BF16, 0)], hidden, swap(hidden), *update)
    return latent


def solution(mesh):
    return jax.shard_map(
        shards,
        mesh=mesh,
        in_specs=(
            P("band", None),
            P("band", None),
            P("band", None),
            P("band", None),
            P("band", None),
            P("band", None),
            P("band"),
            P("band"),
            P(None, "tp"),
            P("tp", None),
            P(None, "tp"),
            P(None, "tp"),
            P("tp", None),
            P(None, "tp"),
            P("tp", None),
            P(None, None, "tp"),
            P(None, None, "tp"),
            P(None, None, "tp"),
            P(None, "tp", None),
            P(None, None, "tp"),
            P(None, "tp", None),
        ),
        out_specs=P("band", None),
        check_vma=False,
    )
```

```python
import functools

import jax
import jax.numpy as jnp
import numpy as np
from jax import lax
from jax.experimental import pallas as pl
from jax.experimental.pallas import tpu as pltpu
from jax.sharding import PartitionSpec as P

BF16 = jnp.bfloat16
F32 = jnp.float32


def matmul(left, right, left_dim=1, right_dim=0):
    dims = (((left_dim,), (right_dim,)), ((), ()))
    return lax.dot_general(left, right, dims, preferred_element_type=F32)


def silu(values):
    half = 0.5 * values
    return half + half * jnp.tanh(half)


def normalize(values, axis):
    centre = jnp.mean(values, axis=axis, keepdims=True)
    centered = values - centre
    variance = jnp.mean(centered * centered, axis=axis, keepdims=True)
    return centered * lax.rsqrt(variance + 1e-05)


def as_column(row):
    return jnp.transpose(jnp.broadcast_to(row, (128, row.shape[1])))


def pick_rows(column, count):
    n = column.shape[0]
    wide = jnp.concatenate([column] * pl.cdiv(count, 128), axis=1)[:, :count]
    lanes = lax.broadcasted_iota(jnp.int32, (n, count), 1)
    return jnp.where(wide == lanes, 1.0, 0.0).astype(BF16)


def pick_columns(row, count):
    n = row.shape[1]
    rows = lax.broadcasted_iota(jnp.int32, (count, n), 0)
    return jnp.where(row == rows, 1.0, 0.0).astype(BF16)


class Carry:
    def __init__(self, array, layer=None, used=False):
        self.array, self.layer, self.used, self.pieces = array, layer, used, 1
        self.shape = array.shape if layer is None else array.shape[1:]


class Layer:
    def __init__(self, array, layer):
        self.array, self.layer = array, layer


class Far:
    def __init__(self, array, layer=None, pieces=1):
        self.array, self.layer, self.pieces = array, layer, pieces
        self.shape = array.shape if layer is None else array.shape[1:]


class Incoming:
    def __init__(self, spec, ref, held, sems, first):
        self.source = ref if spec.layer is None else ref.at[spec.layer]
        self.held, self.sems, self.first = held, sems, first
        self.shape, self.pieces, self.rows = spec.shape, spec.pieces, spec.shape[0] // spec.pieces
        self.waiting = True
        for index in range(self.pieces):
            self.copy(index).start()

    def copy(self, index):
        rows = pl.ds(index * self.rows, self.rows)
        sem = self.sems.at[self.first + index]
        return pltpu.make_async_copy(self.source.at[rows], self.held.at[rows], sem)

    def piece(self, index):
        self.waiting = False
        self.copy(index).wait()
        return self.held[pl.ds(pl.multiple_of(index * self.rows, self.rows), self.rows), :]

    def wait(self):
        if self.waiting:
            self.waiting = False
            for index in range(self.pieces):
                self.copy(index).wait()

    def __getitem__(self, key):
        self.wait()
        return self.held[key]


class Outgoing:
    def __init__(self, ref, held, sems, first, pieces):
        self.ref, self.held, self.sems, self.first = ref, held, sems, first
        self.pieces, self.rows = pieces, ref.shape[0] // pieces

    def copy(self, index):
        rows = pl.ds(index * self.rows, self.rows)
        sem = self.sems.at[self.first + index]
        return pltpu.make_async_copy(self.held.at[rows], self.ref.at[rows], sem)

    def put(self, index, values):
        self.held[pl.ds(pl.multiple_of(index * self.rows, self.rows), self.rows), :] = values
        self.copy(index).start()

    def wait(self):
        for index in range(self.pieces):
            self.copy(index).wait()


def call(kernel, outs, *args, extra=()):
    scratch, semaphores = [], 0
    for arg in args:
        if isinstance(arg, Far):
            scratch.append(pltpu.VMEM(arg.shape, arg.array.dtype))
            semaphores += arg.pieces
    for shape, dtype, pieces in outs:
        if pieces:
            scratch.append(pltpu.VMEM(shape, dtype))
            semaphores += pieces
    carried = [arg for arg in args if isinstance(arg, Carry)]
    semaphores += len(carried)
    all_outs = list(outs) + [(arg.shape, arg.array.dtype, 0) for arg in carried]

    def body(*refs):
        inputs, refs = refs[: len(args)], refs[len(args) :]
        results, held = refs[: len(all_outs)], list(refs[len(all_outs) : -1])
        held, own = held[: len(held) - len(extra)], held[len(held) - len(extra) :]
        sems, first = refs[-1], 0
        copied = list(results[len(outs) :])
        taken, given, carries = [], [], []
        for arg, ref in zip(args, inputs):
            if isinstance(arg, Far):
                taken.append(Incoming(arg, ref, held.pop(0), sems, first))
                first += arg.pieces
            elif isinstance(arg, Carry):
                carries.append((arg, ref, copied.pop(0), first))
                if arg.used:
                    taken.append(Incoming(arg, ref, carries[-1][2], sems, first))
                first += 1
            else:
                taken.append(ref.at[arg.layer] if isinstance(arg, Layer) else ref)
        carries = [Incoming(*each[:3], sems, each[3]) for each in carries if not each[0].used]
        for (shape, dtype, pieces), ref in zip(outs, results):
            if pieces:
                ref = Outgoing(ref, held.pop(0), sems, first, pieces)
                first += pieces
            given.append(ref)
        kernel(*taken, *given, *own)
        for ref in taken + carries + given:
            if isinstance(ref, (Incoming, Outgoing)):
                ref.wait()

    def space(far):
        return pl.BlockSpec(memory_space=pltpu.HBM if far else pltpu.VMEM)

    def operand(arg):
        if isinstance(arg, (Far, Carry)):
            return pltpu.with_memory_space_constraint(arg.array, pltpu.HBM)
        return arg.array if isinstance(arg, Layer) else arg

    return pl.pallas_call(
        body,
        out_shape=[
            pltpu.HBM(shape, dtype) if pieces else jax.ShapeDtypeStruct(shape, dtype)
            for shape, dtype, pieces in all_outs
        ],
        in_specs=[space(isinstance(arg, (Far, Carry))) for arg in args],
        out_specs=[space(pieces > 0) for _, _, pieces in all_outs],
        scratch_shapes=scratch + list(extra) + [pltpu.SemaphoreType.DMA((max(semaphores, 1),))],
        compiler_params=pltpu.CompilerParams(vmem_limit_bytes=32 * 1024 * 1024),
    )(*[operand(arg) for arg in args])


def each_block(count, block, body, init=None, unroll=1):
    def step(index, carry):
        return body(pl.ds(pl.multiple_of(index * block, block), block), index, carry)

    return lax.fori_loop(0, count // block, step, init, unroll=unroll)


def embed_own_kernel(block, x, in_own, own_ref):
    weight = in_own[...]
    x.wait()

    def step(columns, index, carry):
        own_ref[:, columns] = silu(matmul(weight, x[:, columns], 0)).astype(BF16)

    each_block(x.shape[1], block, step)


def embed_kernel(block, x, own, in_other, out_own, out_other, sender_own, sender_other, slots, send_ref,
                 proj_ref):
    half = sender_own.shape[1]

    def embed(columns, index, carry):
        other = silu(matmul(in_other[...], x[:, columns], 0)).astype(BF16)
        total = matmul(out_own[...], own[:, columns], 0) + matmul(out_other[...], other, 0)
        latent = normalize(total, 0).astype(BF16)
        proj_ref[:half, columns] = matmul(sender_own[...], latent, 0).astype(BF16)
        proj_ref[half:, columns] = matmul(sender_other[...], latent, 0).astype(BF16)

    each_block(x.shape[1], block, embed, unroll=True)
    slots.wait()

    def gather(columns, index, carry):
        low = lax.axis_index("tp") == 0
        row = jnp.where(low, slots[2:3, columns], slots[0:1, columns])
        pick = pick_columns(row, proj_ref.shape[1])
        send_ref[:, columns] = matmul(proj_ref[...], pick).astype(BF16)

    each_block(send_ref.shape[1], block, gather, unroll=True)


def join(incoming, row, mesh_proj):
    pick = pick_columns(row, mesh_proj.shape[1])
    active = silu(incoming + matmul(mesh_proj, pick)).astype(BF16)
    return matmul(pick, jnp.transpose(active))


def prepare(latent, msg_own, msg_other, first_own, first_other, base_ref, fold_ref):
    width = latent.shape[1]
    firsts = (first_own, first_other)
    base = jnp.concatenate([matmul(latent, each[:width, :]) for each in firsts], axis=1)
    fold = [
        jnp.concatenate([matmul(msg[...], each[width:, :]) for each in firsts], axis=1)
        for msg in (msg_own, msg_other)
    ]
    fold = jnp.concatenate(fold, axis=0).astype(BF16)
    for values, ref in ((base, base_ref), (fold, fold_ref)):
        if isinstance(ref, Outgoing):
            ref.put(0, values)
        else:
            ref[...] = values


def encode_mid_kernel(latent, receiver_own, receiver_other, grid_slots, mesh_slots, grid_proj,
                      msg_own, msg_other, first_own, first_other, gathered_ref, pick_ref,
                      sum_ref, base_ref, fold_ref, proj_ref):
    nodes = latent[...]
    half = receiver_own.shape[1]
    proj_ref[:half, :] = matmul(receiver_own[...], nodes, 0, 1).astype(BF16)
    proj_ref[half:, :] = matmul(receiver_other[...], nodes, 0, 1).astype(BF16)
    low = lax.axis_index("tp") == 0
    middle = grid_slots.shape[1] // 2
    grid_row, mesh_row = [
        jnp.where(low, each[1:2, :middle], each[1:2, middle:]) for each in (grid_slots, mesh_slots)
    ]
    incoming = matmul(grid_proj[...], pick_columns(grid_row, grid_proj.shape[1]))
    sum_ref[...] = join(incoming, mesh_row, proj_ref[...])
    pick = pick_columns(jnp.where(low, mesh_slots[0:1, :], mesh_slots[2:3, :]), nodes.shape[0])
    pick_ref[...] = pick
    gathered_ref[...] = matmul(proj_ref[...], pick).astype(BF16)
    prepare(nodes, msg_own, msg_other, first_own, first_other, base_ref, fold_ref)


def encode_far_kernel(gathered, pick, partial, arrived, sum_ref):
    active = silu(arrived[...].astype(F32) + gathered[...].astype(F32)).astype(BF16)
    sum_ref[...] = (partial[...] + matmul(pick[...], jnp.transpose(active))).astype(BF16)


def node_kernel(hidden_own, hidden_other, fold, base, second_own, second_other, latent, *refs):
    half = second_own.shape[0]
    own, other = hidden_own[...], hidden_other[...]
    if own.shape[1] > half:
        mine, theirs = own.astype(F32), other.astype(F32)
        own = (mine[:, :half] + theirs[:, half:]).astype(BF16)
        other = (mine[:, half:] + theirs[:, :half]).astype(BF16)
    pre_act = matmul(own, fold[:half, :]) + matmul(other, fold[half:, :])
    inner = silu(base[...] + pre_act).astype(BF16)
    total = matmul(inner[:, :half], second_own[...]) + matmul(inner[:, half:], second_other[...])
    new = (latent[...].astype(F32) + normalize(total, 1)).astype(BF16)
    if len(refs) == 1:
        refs[0][...] = new
        return
    sender_w, halo, new_ref, outgoing_ref = refs
    new_ref.put(0, new)
    local = matmul(new, sender_w[...]).astype(BF16)

    def step(columns, index, carry):
        pick = pick_rows(as_column(halo[:, columns]), local.shape[0])
        outgoing_ref.put(index, matmul(pick, local).astype(BF16))

    each_block(halo.shape[1], outgoing_ref.rows, step, unroll=True)


def edge_near_kernel(latent, sender_w, receiver_w, edge_w, edges, senders, receivers, msg_own,
                     msg_other, first_own, first_other, near_ref, base_ref, fold_ref):
    nodes = latent[...]
    count = nodes.shape[0]
    table = [matmul(each[...], nodes, 0, 1).astype(BF16) for each in (sender_w, receiver_w)]
    table = jnp.concatenate(table, axis=1)
    weight = edge_w[...]

    def step(columns, index, carry):
        pick = jnp.concatenate(
            [pick_columns(each[:, columns], count) for each in (senders, receivers)], axis=0
        )
        near = matmul(weight, edges.piece(index), 0, 1) + matmul(table, pick)
        near_ref.put(index, near.astype(BF16))

    each_block(edges.shape[0], edges.rows, step)
    prepare(nodes, msg_own, msg_other, first_own, first_other, base_ref, fold_ref)


def edge_far_kernel(count, arrived, near, senders, receivers, hidden_ref):
    far = arrived.shape[0]
    table = jnp.transpose(arrived[...])

    def step(columns, index, total):
        pre_act = matmul(table, pick_columns(senders[:, columns] - count, far))
        pre_act = near.piece(index).astype(F32) + pre_act
        pick = pick_columns(receivers[:, columns], count)
        return total + matmul(pick, jnp.transpose(silu(pre_act).astype(BF16)))

    total = each_block(senders.shape[1], near.shape[1], step, jnp.zeros(hidden_ref.shape, F32))
    hidden_ref[...] = total.astype(BF16)


def swap(values):
    return lax.ppermute(values, "tp", [(0, 1), (1, 0)])


def shards(
    grid_input,
    mesh_latent,
    edge_latent,
    slot_grid_row,
    slot_mesh_row,
    halo_send,
    edge_sender,
    edge_receiver,
    embed_in,
    embed_out,
    encode_sender,
    encode_receiver,
    encode_out,
    encode_node_in,
    encode_node_out,
    layer_sender,
    layer_receiver,
    layer_edge,
    layer_message,
    layer_node_in,
    layer_node_out,
):
    nodes, width = mesh_latent.shape
    grid_rows = grid_input.shape[0]
    slot_count = slot_grid_row.shape[1]
    half = encode_sender.shape[1]
    bands, halo_slots = halo_send.shape
    layers = layer_sender.shape[0]
    pieces = 1
    block = 1024
    edge_rows = edge_latent.shape[0] // pieces

    own, x, out_own, sender_own = call(
        functools.partial(embed_own_kernel, block), [((half, grid_rows), BF16, 0)], Carry(grid_input.T, None, True),
        Far(embed_in), Carry(embed_out), Carry(encode_sender),
    )
    outgoing, grid_proj = call(
        functools.partial(embed_kernel, block),
        [((width, slot_count), BF16, 0), ((width, grid_rows), BF16, 0)], x, own, swap(embed_in),
        out_own, swap(embed_out), sender_own, swap(encode_sender), Far(slot_grid_row),
    )
    pairs = [(2 * i, 2 * i + 2) for i in range(bands - 1)]
    pairs += [(2 * i + 3, 2 * i + 1) for i in range(bands - 1)]
    arrived = lax.ppermute(outgoing, ("band", "tp"), pairs)

    owned = (encode_receiver, encode_out, encode_node_in, encode_node_out, layer_message,
             layer_node_in, layer_node_out)
    owned, grid_proj = lax.optimization_barrier((owned, grid_proj))
    receiver, encode_message, encode_first, encode_second, message, first, second = [
        (each, swap(each)) for each in owned
    ]

    def prepare_weights(message, first, layer):
        return [Far(each, layer) for pair in (message, first) for each in pair]

    prepared = [((nodes, width), F32, 1), ((width, width), BF16, 1)]
    gathered, pick, partial, base, fold, *update, sender_w = call(
        encode_mid_kernel,
        [((width, slot_count), BF16, 0), ((nodes, slot_count), BF16, 0), ((nodes, width), F32, 0),
         ((nodes, width), F32, 0), ((width, width), BF16, 0)],
        Far(mesh_latent), Far(receiver[0]), Far(receiver[1]), Far(slot_grid_row),
        Far(slot_mesh_row), grid_proj, *prepare_weights(encode_message, encode_first, None),
        Carry(encode_second[0]), Carry(encode_second[1]), Carry(mesh_latent),
        Carry(layer_sender, 0), extra=[pltpu.VMEM((width, nodes), BF16)],
    )
    (hidden,) = call(
        encode_far_kernel, [((nodes, width), BF16, 0)], gathered, pick, partial, arrived,
    )

    order = (6, 5, 4, 3, 2, 1, 0)
    bits = len(order)
    members = np.arange(bands).reshape((2,) * bits).transpose(order).reshape(-1).tolist()
    halo_row = halo_send.reshape((2,) * bits + (halo_slots,)).transpose(order + (bits,)).reshape(1, -1)
    slot = edge_sender - nodes
    place = slot & (halo_slots - 1)
    for to, bit in enumerate(order):
        place += ((slot // (halo_slots << (bits - 1 - bit))) & 1) * (halo_slots << (bits - 1 - to))
    sender_row = jnp.where(slot < 0, edge_sender, place + nodes).reshape(1, -1)
    receiver_row = edge_receiver.reshape(1, -1)
    update = [fold, base, *update]
    node_out = [((nodes, width), BF16, 1), ((bands * halo_slots, half), BF16, 8)]

    for layer in range(layers):
        latent, outgoing = call(
            node_kernel, node_out, hidden, swap(hidden), *update, sender_w, halo_row
        )
        arrived = lax.all_to_all(
            outgoing.reshape(bands, halo_slots, half), "band", split_axis=0, concat_axis=0,
            axis_index_groups=[members], tiled=True
        ).reshape(bands * halo_slots, half)
        near, base, fold = call(
            edge_near_kernel, [((pieces * half, edge_rows), BF16, pieces)] + prepared, Far(latent),
            Far(layer_sender, layer), Far(layer_receiver, layer), Far(layer_edge, layer),
            Far(edge_latent, None, pieces), sender_row, receiver_row,
            *prepare_weights(message, first, layer),
        )
        (hidden,) = call(
            functools.partial(edge_far_kernel, nodes), [((nodes, half), BF16, 0)], arrived,
            Far(near, None, pieces), sender_row, receiver_row,
        )
        update = [fold, base, Layer(second[0], layer), Layer(second[1], layer), latent]
        if layer + 1 < layers:
            sender_w = Layer(layer_sender, layer + 1)
    (latent,) = call(node_kernel, [((nodes, width), BF16, 0)], hidden, swap(hidden), *update)
    return latent


def solution(mesh):
    return jax.shard_map(
        shards,
        mesh=mesh,
        in_specs=(
            P("band", None),
            P("band", None),
            P("band", None),
            P("band", None),
            P("band", None),
            P("band", None),
            P("band"),
            P("band"),
            P(None, "tp"),
            P("tp", None),
            P(None, "tp"),
            P(None, "tp"),
            P("tp", None),
            P(None, "tp"),
            P("tp", None),
            P(None, None, "tp"),
            P(None, None, "tp"),
            P(None, None, "tp"),
            P(None, "tp", None),
            P(None, None, "tp"),
            P(None, "tp", None),
        ),
        out_specs=P("band", None),
        check_vma=False,
    )
```
